32 devices in a mesh: dp: 4 (over y, core), mp: 8 (over z, x).
Axes of the slice: x: 2, y: 2, z: 4, core: 2. Of those that a mesh axis runs over, the one named last changes fastest.
Arguments:
- features: bfloat16 [4096, 65536], P('dp', 'mp'), may hold values from -6 to 6
- cotangent: bfloat16 [4096, 65536], P('dp', 'mp'), may hold values from -6 to 6
- factor_one: bfloat16 [256, 256, 256], P('mp', 'dp'), may hold values from -0.375 to 0.375
- factor_two: bfloat16 [256, 256, 256], P('mp', 'dp'), may hold values from -0.375 to 0.375
Outputs:
- layer_out: bfloat16 [4096, 65536], P('dp', 'mp')
- grad_input: bfloat16 [4096, 65536], P('dp', 'mp')
- grad_one: float32 [256, 256, 256], P('mp', 'dp')
- grad_two: float32 [256, 256, 256], P('mp', 'dp')
The draws below stay inside these ranges and needn't reach their ends.
All inputs are finite; a program needn't handle non-finite values.
Results may differ from the reference program's by a relative error of at most 0.0095.
Values may be sent and summed in bfloat16 or wider, within the bound.
No kernel may reach another device: no remote copies, remote signals or barrier semaphores. Data moves between devices by JAX's collectives and lax.ppermute only.
A program may use at most 256 MiB of HBM per device.

```python
import math
import jax
import jax.numpy as jnp
from jax import lax

NB = 256
BS = 256
WIDTH = 65536
TOKENS = 4096


def steps_of(rng, shape, shards, smallest, high):
    factor_of, own = 1.0, jax.random.fold_in(rng, 6)
    for position, blocks in shards:
        draws = jnp.exp(jax.random.uniform(jax.random.fold_in(own, position), (blocks,), jnp.float32, smallest / len(shards), high / len(shards)))
        factor_of = factor_of * jnp.repeat(draws, shape[position] // blocks).reshape([-1 if axis == position else 1 for axis in range(len(shape))])
    return factor_of


def noise(key, dims, scale, bound, cuts=(), held_as=jnp.bfloat16):
    result = scale * jax.random.normal(key, dims, jnp.float32)
    if cuts:
        result = result * steps_of(key, dims, cuts, -0.22, 0.18)
    return jnp.clip(result, -bound, bound).astype(held_as)


def setup_inputs(seed: int = 0) -> dict:
    keys = jax.random.split(jax.random.key(seed), 5)
    features = noise(keys[0], (TOKENS, WIDTH), 1.0, 6.0, ((0, 4), (1, 8)))
    cotangent = noise(keys[1], (TOKENS, WIDTH), 1.0, 6.0, ((0, 4), (1, 8)))
    factor_one = noise(keys[2], (NB, BS, BS), BS ** -0.5, 0.375, ((0, 8), (1, 4)))
    factor_two = noise(keys[3], (BS, NB, NB), NB ** -0.5, 0.375, ((0, 8), (1, 4)))
    return dict(features=features, cotangent=cotangent, factor_one=factor_one, factor_two=factor_two)


def gelu_value(value):
    inner = math.sqrt(2.0 / math.pi) * (value + 0.044715 * value * value * value)
    return 0.5 * value * (1.0 + jnp.tanh(inner))

def gelu_slope(value):
    scale = math.sqrt(2.0 / math.pi)
    tangent = jnp.tanh(scale * (value + 0.044715 * value * value * value))
    return 0.5 * (1.0 + tangent) + 0.5 * value * (1.0 - tangent * tangent) * scale * (1.0 + 3.0 * 0.044715 * value * value)

def reference(features, cotangent, factor_one, factor_two):
    block_rows = 512 if TOKENS % 512 == 0 else TOKENS
    count = TOKENS // block_rows
    w_one = factor_one.astype(jnp.float32)
    w_two = factor_two.astype(jnp.float32)

    def advance(carry, pair):
        rows_in, rows_cot = pair
        blocks_in = rows_in.reshape(block_rows, NB, BS).astype(jnp.float32)
        first = jnp.einsum('tbi,bij->tbj', blocks_in, w_one).astype(jnp.bfloat16)
        preact = jnp.einsum('tbj,jbk->tjk', first.astype(jnp.float32), w_two)
        layer_out = (rows_in.astype(jnp.float32) + gelu_value(preact).reshape(block_rows, -1)).astype(jnp.bfloat16)
        cot_blocks = rows_cot.astype(jnp.float32).reshape(block_rows, BS, NB)
        slope = (cot_blocks * gelu_slope(preact)).astype(jnp.bfloat16)
        back_first = jnp.einsum('tjk,jbk->tbj', slope.astype(jnp.float32), w_two).astype(jnp.bfloat16)
        grad_input = (rows_cot.astype(jnp.float32) + jnp.einsum('tbj,bij->tbi', back_first.astype(jnp.float32), w_one).reshape(block_rows, -1)).astype(jnp.bfloat16)
        grad_one = carry[0] + jnp.einsum('tbi,tbj->bij', blocks_in, back_first.astype(jnp.float32))
        grad_two = carry[1] + jnp.einsum('tbj,tjk->jbk', first.astype(jnp.float32), slope.astype(jnp.float32))
        return ((grad_one, grad_two), (layer_out, grad_input))
    start = (jnp.zeros((NB, BS, BS), jnp.float32), jnp.zeros((BS, NB, NB), jnp.float32))
    stacked = (features.reshape(count, block_rows, NB * BS), cotangent.reshape(count, block_rows, NB * BS))
    grads, outputs = lax.scan(advance, start, stacked)
    layer_out = outputs[0].reshape(TOKENS, NB * BS)
    grad_input = outputs[1].reshape(TOKENS, NB * BS)
    return (layer_out, grad_input, grads[0], grads[1])
```

```python
import functools
import math

import jax
import jax.numpy as jnp
from jax import lax
from jax.experimental import pallas as pl
from jax.experimental.pallas import tpu as pltpu
from jax.sharding import PartitionSpec as P

LANES = 128
VMEM_LIMIT = 56 * 1024 * 1024
GELU_SCALE = math.sqrt(2.0 / math.pi)


def contract(left, right, left_axis, right_axis):
    return lax.dot_general(
        left, right, (((left_axis,), (right_axis,)), ((), ())), preferred_element_type=jnp.float32
    )


def first_kernel(width, owners, held, cuts, pieces, *refs):
    feat_ref, w_refs = refs[0], refs[1 : 1 + pieces]
    out_refs, swap = refs[1 + pieces : -1], refs[-1]
    group = w_refs[0].shape[0]
    tokens = feat_ref.shape[0]
    for piece in range(pieces):
        for b in range(group):
            column = (piece * group + b) * width
            rows = contract(w_refs[piece][b], feat_ref[:, column : column + width], 0, 1)
            for lane in range(tokens // LANES):
                swap[lane, pl.ds(b, width, stride=group), :] = rows[
                    :, lane * LANES : (lane + 1) * LANES
                ]
        for out_ref, (low, high) in zip(out_refs, cuts):
            for owner in range(owners):
                start = (owner * held + low) * group
                for lane in range(tokens // LANES):
                    block = swap[lane, pl.ds(start, (high - low) * group), :]
                    out_ref[
                        owner,
                        :,
                        piece * group : (piece + 1) * group,
                        lane * LANES : (lane + 1) * LANES,
                    ] = block.reshape(high - low, group, LANES).astype(jnp.bfloat16)


def first_parts(features, weights, cuts, owners, held, start_piece):
    tokens = features.shape[0]
    group, width, _ = weights[0].shape
    pieces = len(weights)
    tile = min(256, tokens)
    flops = 2 * tokens * pieces * group * width * width
    outs = [
        jax.ShapeDtypeStruct((owners, high - low, pieces * group, tokens), jnp.bfloat16)
        for low, high in cuts
    ]
    moved = 2 * (tokens * pieces * group * width + pieces * group * width * width)
    moved += sum(2 * math.prod(out.shape) for out in outs)
    return pl.pallas_call(
        functools.partial(first_kernel, width, owners, held, cuts, pieces),
        grid=(tokens // tile,),
        in_specs=[pl.BlockSpec((tile, pieces * group * width), lambda t: (t, start_piece))]
        + [pl.BlockSpec((group, width, width), lambda t: (0, 0, 0))] * pieces,
        out_specs=[
            pl.BlockSpec((owners, high - low, pieces * group, tile), lambda t: (0, 0, 0, t))
            for low, high in cuts
        ],
        out_shape=outs,
        scratch_shapes=[pltpu.VMEM((tile // LANES, width * group, LANES), jnp.float32)],
        compiler_params=pltpu.CompilerParams(vmem_limit_bytes=VMEM_LIMIT),
        cost_estimate=pl.CostEstimate(flops=flops, bytes_accessed=moved, transcendentals=0),
        name="first",
    )(features, *weights)


def middle_kernel(owners, held, sources, backs, tile, chained, *refs):
    r_refs = refs[:sources]
    w_ref, feat_ref, cot_ref = refs[sources : sources + 3]
    outs = refs[sources + 3 + chained :]
    layer_ref, part_ref, back_refs = outs[0], outs[1], outs[2:]
    weight = w_ref[0]
    tokens = feat_ref.shape[0]
    part = None
    for begin in range(0, tokens, tile):
        span = slice(begin, begin + tile)
        first = jnp.concatenate([ref[:, 0, :, span] for ref in r_refs], axis=1)
        first = first.reshape(owners * held, tile)
        value = contract(first, weight, 0, 0)
        square = value * value
        tangent = jnp.tanh(GELU_SCALE * (value + 0.044715 * square * value))
        half = 0.5 * (1.0 + tangent)
        layer_ref[span, :] = (feat_ref[span, :].astype(jnp.float32) + value * half).astype(
            jnp.bfloat16
        )
        rate = half + 0.5 * value * (1.0 - tangent * tangent) * GELU_SCALE * (
            1.0 + 3.0 * 0.044715 * square
        )
        slope = (cot_ref[span, :].astype(jnp.float32) * rate).astype(jnp.bfloat16)
        back = contract(weight, slope, 1, 1).astype(jnp.bfloat16).reshape(owners, held, tile)
        size = held // backs
        for index, back_ref in enumerate(back_refs):
            back_ref[:, 0, :, span] = back[:, index * size : (index + 1) * size]
        term = contract(first, slope, 1, 0)
        part = term if part is None else part + term
    part_ref[0] = part.astype(jnp.bfloat16)


def middle_part(received, w_two, features, cotangent, layer, low, backs):
    tokens, columns = features.shape
    owners, count = received[0].shape[:2]
    held = sum(array.shape[2] for array in received)
    depth, width = w_two.shape[1:]
    tile = min(256, tokens)
    chained = 0 if layer is None else 1
    column = pl.BlockSpec((tokens, width), lambda j: (0, low + j))
    size = held // backs
    operands = [*received, w_two, features, cotangent] + ([layer] if chained else [])
    return pl.pallas_call(
        functools.partial(middle_kernel, owners, held, len(received), backs, tile, chained),
        grid=(count,),
        in_specs=[
            pl.BlockSpec((owners, 1, array.shape[2], tokens), lambda j: (0, j, 0, 0))
            for array in received
        ]
        + [pl.BlockSpec((1, depth, width), lambda j: (low + j, 0, 0)), column, column]
        + [pl.BlockSpec(memory_space=pl.ANY)] * chained,
        out_specs=[column, pl.BlockSpec((1, depth, width), lambda j: (j, 0, 0))]
        + [pl.BlockSpec((owners, 1, size, tokens), lambda j: (0, j, 0, 0))] * backs,
        out_shape=[
            jax.ShapeDtypeStruct((tokens, columns), jnp.bfloat16),
            jax.ShapeDtypeStruct((count, depth, width), jnp.bfloat16),
        ]
        + [jax.ShapeDtypeStruct((owners, count, size, tokens), jnp.bfloat16)] * backs,
        input_output_aliases={len(operands) - 1: 0} if chained else {},
        compiler_params=pltpu.CompilerParams(vmem_limit_bytes=VMEM_LIMIT),
        cost_estimate=pl.CostEstimate(
            flops=6 * count * tokens * depth * width,
            bytes_accessed=count * (10 * tokens * width + 4 * depth * width),
            transcendentals=count * tokens * width,
        ),
        name="middle",
    )(*operands)


def last_kernel(owners, held, cuts, chained, *refs):
    count = len(cuts)
    q_refs = refs[:count]
    w_ref, feat_ref, cot_ref = refs[count : count + 3]
    grad_ref, part_ref, swap, total = refs[count + 3 + chained :]
    group, width, _ = w_ref.shape
    tokens = feat_ref.shape[0]
    lanes = tokens // LANES
    step = pl.program_id(0)

    @pl.when(step == 0)
    def _():
        total[...] = jnp.zeros_like(total)

    for q_ref, (low, high) in zip(q_refs, cuts):
        for owner in range(owners):
            start = (owner * held + low) * group
            for lane in range(lanes):
                block = q_ref[owner, :, :, lane * LANES : (lane + 1) * LANES]
                swap[lane, pl.ds(start, (high - low) * group), :] = block.astype(
                    jnp.float32
                ).reshape((high - low) * group, LANES)
    for b in range(group):
        back = jnp.concatenate(
            [swap[lane, pl.ds(b, owners * held, stride=group), :] for lane in range(lanes)], axis=1
        ).astype(jnp.bfloat16)
        columns = slice(b * width, (b + 1) * width)
        through = contract(back, w_ref[b], 0, 1)
        grad_ref[:, columns] = (cot_ref[:, columns].astype(jnp.float32) + through).astype(
            jnp.bfloat16
        )
        total[b] += contract(back, feat_ref[:, columns], 1, 0)

    @pl.when(step == pl.num_programs(0) - 1)
    def _():
        for b in range(group):
            part_ref[b] = total[b].T.astype(jnp.bfloat16)


def last_part(returned, cuts, w_one, features, cotangent, grad, piece):
    tokens, columns = features.shape
    group, width, _ = w_one.shape
    owners = returned[0][0].shape[0]
    held = max(high for _, high in cuts)
    tile = min(256, tokens)
    chained = 0 if grad is None else 1
    strip = pl.BlockSpec((tile, group * width), lambda t: (t, piece))
    operands = [array for array, _ in returned] + [w_one, features, cotangent]
    operands += [grad] if chained else []

    def q_spec(array, at):
        return pl.BlockSpec((owners, array.shape[1], group, tile), lambda t: (0, 0, at, t))

    return pl.pallas_call(
        functools.partial(last_kernel, owners, held, cuts, chained),
        grid=(tokens // tile,),
        in_specs=[q_spec(array, at) for array, at in returned]
        + [pl.BlockSpec((group, width, width), lambda t: (0, 0, 0)), strip, strip]
        + [pl.BlockSpec(memory_space=pl.ANY)] * chained,
        out_specs=[strip, pl.BlockSpec((group, width, width), lambda t: (0, 0, 0))],
        out_shape=[
            jax.ShapeDtypeStruct((tokens, columns), jnp.bfloat16),
            jax.ShapeDtypeStruct((group, width, width), jnp.bfloat16),
        ],
        input_output_aliases={len(operands) - 1: 0} if chained else {},
        scratch_shapes=[
            pltpu.VMEM((tile // LANES, owners * held * group, LANES), jnp.float32),
            pltpu.VMEM((group, width, width), jnp.float32),
        ],
        compiler_params=pltpu.CompilerParams(vmem_limit_bytes=VMEM_LIMIT),
        cost_estimate=pl.CostEstimate(
            flops=4 * group * tokens * width * width,
            bytes_accessed=group * (8 * tokens * width + 4 * width * width),
            transcendentals=0,
        ),
        name="last",
    )(*operands)


def exchange(array):
    return lax.all_to_all(array, "mp", split_axis=0, concat_axis=0, tiled=True)


def scatter(part):
    return lax.psum_scatter(part, "dp", scatter_dimension=1, tiled=True)


def on_device(features, cotangent, factor_one, factor_two):
    owners = lax.axis_size("mp")
    held = factor_one.shape[0]
    group = min(16, held)
    pieces = held // group
    quarter = held // 4
    cuts = [(0, quarter), (quarter, 2 * quarter), (2 * quarter, held)]

    w_one = [
        lax.all_gather(factor_one[p * group : (p + 1) * group], "dp", axis=1, tiled=True)
        for p in range(pieces)
    ]
    w_two = lax.all_gather(factor_two, "dp", axis=1, tiled=True)

    head = [
        exchange(first_parts(features, [w_one[p]], cuts[:1], owners, held, p)[0])
        for p in range(pieces)
    ]
    rest = first_parts(features, w_one, cuts[1:], owners, held, 0)
    received = [head] + [[exchange(array)] for array in rest]

    layer, parts_two, returned = None, [], []
    for index, (low, _) in enumerate(cuts):
        final = index == len(cuts) - 1
        layer, part, *backs = middle_part(
            received[index], w_two, features, cotangent, layer, low, pieces if final else 1
        )
        parts_two.append(scatter(part))
        returned.append([exchange(back) for back in backs])

    grad, parts_one = None, []
    for p in range(pieces):
        arrays = [(returned[0][0], p), (returned[1][0], p), (returned[2][p], 0)]
        grad, part = last_part(arrays, cuts, w_one[p], features, cotangent, grad, p)
        parts_one.append(scatter(part))
    return (
        layer,
        grad,
        jnp.concatenate(parts_one, axis=0).astype(jnp.float32),
        jnp.concatenate(parts_two, axis=0).astype(jnp.float32),
    )


def solution(mesh):
    in_specs = (P("dp", "mp"), P("dp", "mp"), P("mp", "dp", None), P("mp", "dp", None))
    out_specs = (P("dp", "mp"), P("dp", "mp"), P("mp", "dp", None), P("mp", "dp", None))
    return jax.shard_map(
        on_device, mesh=mesh, in_specs=in_specs, out_specs=out_specs, check_vma=False
    )
```

```python
import functools
import math

import jax
import jax.numpy as jnp
from jax import lax
from jax.experimental import pallas as pl
from jax.experimental.pallas import tpu as pltpu
from jax.sharding import PartitionSpec as P

LANES = 128
VMEM_LIMIT = 60 * 1024 * 1024
GELU_SCALE = math.sqrt(2.0 / math.pi)


def contract(left, right, left_axis, right_axis):
    return lax.dot_general(
        left, right, (((left_axis,), (right_axis,)), ((), ())), preferred_element_type=jnp.float32
    )


def first_rows(feat_ref, weight, out_refs, cuts, owners, held, group, width, swap):
    tokens = feat_ref.shape[0]
    for b in range(group):
        rows = contract(weight[b], feat_ref[:, b * width : (b + 1) * width], 0, 1)
        for lane in range(tokens // LANES):
            swap[lane, pl.ds(b, width, stride=group), :] = rows[
                :, lane * LANES : (lane + 1) * LANES
            ]
    for out_ref, (low, high) in zip(out_refs, cuts):
        for owner in range(owners):
            start = (owner * held + low) * group
            for lane in range(tokens // LANES):
                block = swap[lane, pl.ds(start, (high - low) * group), :]
                out_ref[owner, :, :, lane * LANES : (lane + 1) * LANES] = block.reshape(
                    high - low, group, LANES
                ).astype(jnp.bfloat16)


def first_kernel(cuts, owners, held, feat_ref, w_ref, *refs):
    group, width, _ = w_ref.shape
    first_rows(feat_ref, w_ref, refs[:-1], cuts, owners, held, group, width, refs[-1])


def head_kernel(cuts, owners, held, shares, position_ref, feat_ref, *refs):
    part_refs, weight, swap = refs[:shares], refs[-2], refs[-1]
    group, width, _ = weight.shape
    rows = width // shares

    @pl.when(pl.program_id(0) == 0)
    def _():
        for step, part_ref in enumerate(part_refs):
            place = pl.multiple_of((position_ref[0] ^ step) * rows, rows)
            weight[:, pl.ds(place, rows), :] = part_ref[...]

    first_rows(feat_ref, weight, refs[shares:-2], cuts, owners, held, group, width, swap)


def first_parts(features, weights, position, cuts, owners, held, group, piece):
    tokens = features.shape[0]
    width = weights[0].shape[2]
    shares = len(weights)
    tile = min(256, tokens)
    outs = [
        jax.ShapeDtypeStruct((owners, high - low, group, tokens), jnp.bfloat16)
        for low, high in cuts
    ]
    moved = 2 * (tokens * group * width + group * width * width)
    moved += sum(2 * math.prod(out.shape) for out in outs)
    swap = pltpu.VMEM((tile // LANES, width * group, LANES), jnp.float32)
    params = dict(
        out_shape=outs,
        compiler_params=pltpu.CompilerParams(vmem_limit_bytes=VMEM_LIMIT),
        cost_estimate=pl.CostEstimate(
            flops=2 * tokens * group * width * width, bytes_accessed=moved, transcendentals=0
        ),
        name="first",
    )
    feat_spec = pl.BlockSpec((tile, group * width), lambda t, *_: (t, piece))
    out_specs = [
        pl.BlockSpec((owners, high - low, group, tile), lambda t, *_: (0, 0, 0, t))
        for low, high in cuts
    ]
    if shares == 1:
        return pl.pallas_call(
            functools.partial(first_kernel, cuts, owners, held),
            grid=(tokens // tile,),
            in_specs=[feat_spec, pl.BlockSpec((group, width, width), lambda t: (piece, 0, 0))],
            out_specs=out_specs,
            scratch_shapes=[swap],
            **params,
        )(features, *weights)
    part_spec = pl.BlockSpec((group, width // shares, width), lambda t, *_: (0, 0, 0))
    return pl.pallas_call(
        functools.partial(head_kernel, cuts, owners, held, shares),
        grid_spec=pltpu.PrefetchScalarGridSpec(
            num_scalar_prefetch=1,
            grid=(tokens // tile,),
            in_specs=[feat_spec] + [part_spec] * shares,
            out_specs=out_specs,
            scratch_shapes=[pltpu.VMEM((group, width, width), jnp.bfloat16), swap],
        ),
        **params,
    )(position, features, *weights)


def middle_kernel(owners, held, sources, groups, tile, chained, *refs):
    r_refs = refs[:sources]
    w_ref, feat_ref, cot_ref = refs[sources : sources + 3]
    outs = refs[sources + 3 + chained :]
    layer_ref, part_ref, back_refs = outs[0], outs[1], outs[2:]
    weight = w_ref[0]
    tokens = feat_ref.shape[0]
    part = None
    for begin in range(0, tokens, tile):
        span = slice(begin, begin + tile)
        first = jnp.concatenate([ref[:, 0, :, span] for ref in r_refs], axis=1)
        first = first.reshape(owners * held, tile)
        value = contract(first, weight, 0, 0)
        square = value * value
        tangent = jnp.tanh(GELU_SCALE * (value + 0.044715 * square * value))
        half = 0.5 * (1.0 + tangent)
        layer_ref[span, :] = (feat_ref[span, :].astype(jnp.float32) + value * half).astype(
            jnp.bfloat16
        )
        rate = half + 0.5 * value * (1.0 - tangent * tangent) * GELU_SCALE * (
            1.0 + 3.0 * 0.044715 * square
        )
        slope = (cot_ref[span, :].astype(jnp.float32) * rate).astype(jnp.bfloat16)
        back = contract(weight, slope, 1, 1).reshape(owners, held, tile)
        start = 0
        for size, back_ref in zip(groups, back_refs):
            back_ref[:, 0, :, span] = back[:, start : start + size].astype(jnp.bfloat16)
            start += size
        term = contract(first, slope, 1, 0)
        part = term if part is None else part + term
    part_ref[0] = part.astype(jnp.bfloat16)


def middle_part(received, w_two, features, cotangent, layer, low, high, groups):
    tokens, columns = features.shape
    owners = received[0][0].shape[0]
    held, count = sum(groups), high - low
    depth, width = w_two.shape[1:]
    tile = min(256, tokens)
    chained = 0 if layer is None else 1
    column = pl.BlockSpec((tokens, width), lambda j: (0, low + j))
    operands = [array for array, _ in received] + [w_two, features, cotangent]
    operands += [layer] if chained else []

    def r_spec(array, skipped):
        return pl.BlockSpec(
            (owners, 1, array.shape[2], tokens), lambda j: (0, low - skipped + j, 0, 0)
        )

    return pl.pallas_call(
        functools.partial(middle_kernel, owners, held, len(received), groups, tile, chained),
        grid=(count,),
        in_specs=[r_spec(array, skipped) for array, skipped in received]
        + [pl.BlockSpec((1, depth, width), lambda j: (low + j, 0, 0)), column, column]
        + [pl.BlockSpec(memory_space=pl.ANY)] * chained,
        out_specs=[column, pl.BlockSpec((1, depth, width), lambda j: (j, 0, 0))]
        + [pl.BlockSpec((owners, 1, size, tokens), lambda j: (0, j, 0, 0)) for size in groups],
        out_shape=[
            jax.ShapeDtypeStruct((tokens, columns), jnp.bfloat16),
            jax.ShapeDtypeStruct((count, depth, width), jnp.bfloat16),
        ]
        + [jax.ShapeDtypeStruct((owners, count, size, tokens), jnp.bfloat16) for size in groups],
        input_output_aliases={len(operands) - 1: 0} if chained else {},
        compiler_params=pltpu.CompilerParams(vmem_limit_bytes=VMEM_LIMIT),
        cost_estimate=pl.CostEstimate(
            flops=6 * count * tokens * depth * width,
            bytes_accessed=count * (10 * tokens * width + 4 * depth * width),
            transcendentals=count * tokens * width,
        ),
        name="middle",
    )(*operands)


def last_kernel(owners, held, sources, shares, chained, *refs):
    count = len(sources)
    q_refs = refs[:count]
    w_ref, feat_ref, cot_ref = refs[count : count + 3]
    grad_ref, part_ref, swap, total = refs[count + 3 + chained :]
    group, width, _ = w_ref.shape
    tokens = feat_ref.shape[0]
    lanes = tokens // LANES
    step = pl.program_id(0)

    @pl.when(step == 0)
    def _():
        total[...] = jnp.zeros_like(total)

    for q_ref, (low, high, skipped) in zip(q_refs, sources):
        for owner in range(owners):
            start = (owner * held + low) * group
            for lane in range(lanes):
                block = q_ref[owner, :, :, lane * LANES : (lane + 1) * LANES].astype(jnp.float32)
                swap[lane, pl.ds(start, (high - low) * group), :] = block[
                    :, skipped : skipped + group
                ].reshape((high - low) * group, LANES)
    for b in range(group):
        back = jnp.concatenate(
            [swap[lane, pl.ds(b, owners * held, stride=group), :] for lane in range(lanes)], axis=1
        ).astype(jnp.bfloat16)
        columns = slice(b * width, (b + 1) * width)
        through = contract(back, w_ref[b], 0, 1)
        grad_ref[:, columns] = (cot_ref[:, columns].astype(jnp.float32) + through).astype(
            jnp.bfloat16
        )
        total[b] += contract(back, feat_ref[:, columns], 1, 0)

    @pl.when(step == pl.num_programs(0) - 1)
    def _():
        rows = width // shares
        for b in range(group):
            part = total[b].T.astype(jnp.bfloat16)
            for share in range(shares):
                part_ref[share, b] = part[share * rows : (share + 1) * rows]


def last_part(returned, start, group, w_one, features, cotangent, grad, shares):
    tokens, columns = features.shape
    width = w_one.shape[1]
    owners = returned[0][0].shape[0]
    tile = min(256, tokens)
    chained = 0 if grad is None else 1
    piece = start // group
    strip = pl.BlockSpec((tile, group * width), lambda t: (t, piece))
    operands = [array for array, _, _ in returned] + [w_one, features, cotangent]
    operands += [grad] if chained else []
    specs, sources, held = [], [], 0
    for array, begin, rows in returned:
        at = (start - begin) // rows
        specs.append(
            pl.BlockSpec(
                (owners, array.shape[1], rows, tile), functools.partial(lambda at, t: (0, 0, at, t), at)
            )
        )
        sources.append((held, held + array.shape[1], (start - begin) % rows))
        held += array.shape[1]
    return pl.pallas_call(
        functools.partial(last_kernel, owners, held, tuple(sources), shares, chained),
        grid=(tokens // tile,),
        in_specs=specs
        + [pl.BlockSpec((group, width, width), lambda t: (piece, 0, 0)), strip, strip]
        + [pl.BlockSpec(memory_space=pl.ANY)] * chained,
        out_specs=[
            strip,
            pl.BlockSpec((shares, group, width // shares, width), lambda t: (0, 0, 0, 0)),
        ],
        out_shape=[
            jax.ShapeDtypeStruct((tokens, columns), jnp.bfloat16),
            jax.ShapeDtypeStruct((shares, group, width // shares, width), jnp.bfloat16),
        ],
        input_output_aliases={len(operands) - 1: 0} if chained else {},
        scratch_shapes=[
            pltpu.VMEM((tile // LANES, owners * held * group, LANES), jnp.float32),
            pltpu.VMEM((group, width, width), jnp.float32),
        ],
        compiler_params=pltpu.CompilerParams(vmem_limit_bytes=VMEM_LIMIT),
        cost_estimate=pl.CostEstimate(
            flops=4 * group * tokens * width * width,
            bytes_accessed=group * (8 * tokens * width + 4 * width * width),
            transcendentals=0,
        ),
        name="last",
    )(*operands)


def exchange(array, before=None):
    if before is not None:
        array = after(array, before)
    return lax.all_to_all(array, "mp", split_axis=0, concat_axis=0, tiled=True)


def after(array, before):
    return lax.optimization_barrier((array, before))[0]


def swap_with(array, step):
    size = lax.axis_size("dp")
    return lax.ppermute(array, "dp", [(d, d ^ step) for d in range(size)])


def gathered_parts(part):
    parts = [part]
    step = lax.axis_size("dp") // 2
    while step:
        came = [swap_with(array, step) for array in parts]
        parts = [array for pair in zip(parts, came) for array in pair]
        step //= 2
    return parts


def scattered_terms(parts):
    me = lax.axis_index("dp")
    take = lambda step: lax.dynamic_index_in_dim(parts, me ^ step, 0, keepdims=False)
    return [take(0)] + [swap_with(take(step), step) for step in range(1, parts.shape[0])]


def scatter(part):
    return lax.psum_scatter(part, "dp", scatter_dimension=1, tiled=True)


def on_device(features, cotangent, factor_one, factor_two):
    owners = lax.axis_size("mp")
    shares = lax.axis_size("dp")
    held = factor_one.shape[0]
    half = held // 2
    split = held % 32 == 0
    piece = half if split else held
    groups = (held // 2, held // 4, held // 4) if split else (held,)

    position = jnp.full((1,), lax.axis_index("dp"), jnp.int32)
    parts = gathered_parts(factor_one[:piece])
    w_one = lax.all_gather(after(factor_one, parts[-1]), "dp", axis=1, tiled=True)
    w_two = lax.all_gather(after(factor_two, w_one), "dp", axis=1, tiled=True)

    head = first_parts(features, parts, position, [(0, held)], owners, held, piece, 0)
    latest = arrived = exchange(head[0])
    received = [[(arrived, 0)], [(arrived, 0)]]
    if split:
        rest = first_parts(
            after(features, head[0]), [w_one], None, [(0, half), (half, held)], owners, held, piece, 1
        )
        for index, array in enumerate(rest):
            latest = exchange(array, latest)
            received[index].append((latest, index * half))

    layer, part_low, back_low = middle_part(
        received[0], w_two, features, cotangent, None, 0, half, (held,)
    )
    latest = back_low = exchange(back_low, latest)
    layer, part_high, *backs = middle_part(
        received[1], w_two, features, cotangent, layer, half, held, groups
    )
    parts_two = [scatter(part_low), scatter(part_high)]

    grad, parts_one, start, sent = None, [], 0, []
    for index, group in enumerate(groups):
        while len(sent) < min(index + 2, len(groups)):
            latest = exchange(backs[len(sent)], (latest, grad) if index else latest)
            sent.append(latest)
        back = after(sent[index], parts_one) if index == 2 else sent[index]
        returned = [(back_low, 0, piece), (back, start, group)]
        grad, part = last_part(
            returned, start, group, w_one, features, cotangent, grad, shares
        )
        terms = [term.astype(jnp.float32) for term in scattered_terms(part)]
        parts_one.append(sum(terms[1:], terms[0]))
        start += group
    return (
        layer,
        grad,
        jnp.concatenate(parts_one, axis=0),
        jnp.concatenate(parts_two, axis=0).astype(jnp.float32),
    )


def solution(mesh):
    in_specs = (P("dp", "mp"), P("dp", "mp"), P("mp", "dp", None), P("mp", "dp", None))
    out_specs = (P("dp", "mp"), P("dp", "mp"), P("mp", "dp", None), P("mp", "dp", None))
    return jax.shard_map(
        on_device, mesh=mesh, in_specs=in_specs, out_specs=out_specs, check_vma=False
    )
```

```python
import functools
import math

import jax
import jax.numpy as jnp
from jax import lax
from jax.experimental import pallas as pl
from jax.experimental.pallas import tpu as pltpu
from jax.sharding import PartitionSpec as P

LANES = 128
VMEM_LIMIT = 60 * 1024 * 1024
GELU_SCALE = math.sqrt(2.0 / math.pi)


def contract(left, right, left_axis, right_axis):
    return lax.dot_general(
        left, right, (((left_axis,), (right_axis,)), ((), ())), preferred_element_type=jnp.float32
    )


def first_rows(feat_ref, weight, out_refs, unit, cuts, owners, held, swap):
    tokens = feat_ref.shape[0]
    group, width, _ = weight.shape
    for b in range(group):
        rows = contract(weight[b], feat_ref[:, b * width : (b + 1) * width], 0, 1)
        for lane in range(tokens // LANES):
            swap[lane, pl.ds(b, width, stride=group), :] = rows[
                :, lane * LANES : (lane + 1) * LANES
            ]
    for out_ref, (low, high) in zip(out_refs, cuts):
        for owner in range(owners):
            start = (owner * held + low) * group
            for lane in range(tokens // LANES):
                block = swap[lane, pl.ds(start, (high - low) * group), :]
                out_ref[owner, unit, :, :, lane * LANES : (lane + 1) * LANES] = block.reshape(
                    high - low, group, LANES
                ).astype(jnp.bfloat16)


def first_kernel(cuts, owners, held, units, *refs):
    feat_refs, w_refs, out_refs = refs[:units], refs[units : 2 * units], refs[2 * units : -1]
    for unit in range(units):
        first_rows(feat_refs[unit], w_refs[unit], out_refs, unit, cuts, owners, held, refs[-1])


def head_kernel(cuts, owners, held, shares, position_ref, feat_ref, *refs):
    part_refs, weight, swap = refs[:shares], refs[-2], refs[-1]
    rows = weight.shape[1] // shares

    @pl.when(pl.program_id(0) == 0)
    def _():
        for step, part_ref in enumerate(part_refs):
            start = pl.multiple_of((position_ref[0] ^ step) * rows, rows)
            weight[:, pl.ds(start, rows), :] = part_ref[...]

    first_rows(feat_ref, weight, refs[shares:-2], 0, cuts, owners, held, swap)


def first_call(features, group, width, cuts, owners, begin, units):
    tokens = features.shape[0]
    tile = min(256, tokens)
    outs = [
        jax.ShapeDtypeStruct((owners, units, high - low, group, tokens), jnp.bfloat16)
        for low, high in cuts
    ]
    moved = 2 * units * (tokens * group * width + group * width * width)
    moved += sum(2 * math.prod(out.shape) for out in outs)
    feat_specs = [
        pl.BlockSpec((tile, group * width), functools.partial(lambda u, t, *_: (t, u), begin + u))
        for u in range(units)
    ]
    out_specs = [
        pl.BlockSpec((owners, units, high - low, group, tile), lambda t, *_: (0, 0, 0, 0, t))
        for low, high in cuts
    ]
    swap = pltpu.VMEM((tile // LANES, width * group, LANES), jnp.float32)
    params = dict(
        out_shape=outs,
        compiler_params=pltpu.CompilerParams(vmem_limit_bytes=VMEM_LIMIT),
        cost_estimate=pl.CostEstimate(
            flops=2 * units * tokens * group * width * width,
            bytes_accessed=moved,
            transcendentals=0,
        ),
        name="first",
    )
    return (tokens // tile,), feat_specs, out_specs, swap, params


def first_parts(features, w_one, group, cuts, owners, held, begin, units):
    width = w_one.shape[1]
    grid, feat_specs, out_specs, swap, params = first_call(
        features, group, width, cuts, owners, begin, units
    )
    w_specs = [
        pl.BlockSpec((group, width, width), functools.partial(lambda u, t: (u, 0, 0), begin + u))
        for u in range(units)
    ]
    return pl.pallas_call(
        functools.partial(first_kernel, cuts, owners, held, units),
        grid=grid,
        in_specs=feat_specs + w_specs,
        out_specs=out_specs,
        scratch_shapes=[swap],
        **params,
    )(*[features] * units, *[w_one] * units)


def first_head(position, features, parts, cuts, owners, held):
    group, rows, width = parts[0].shape
    shares = len(parts)
    grid, feat_specs, out_specs, swap, params = first_call(
        features, group, width, cuts, owners, 0, 1
    )
    return pl.pallas_call(
        functools.partial(head_kernel, cuts, owners, held, shares),
        grid_spec=pltpu.PrefetchScalarGridSpec(
            num_scalar_prefetch=1,
            grid=grid,
            in_specs=feat_specs
            + [pl.BlockSpec((group, rows, width), lambda t, _: (0, 0, 0))] * shares,
            out_specs=out_specs,
            scratch_shapes=[pltpu.VMEM((group, width, width), jnp.bfloat16), swap],
        ),
        **params,
    )(position, features, *parts)


def middle_kernel(owners, group, sources, backs, tile, chained, *refs):
    r_refs = refs[: len(sources)]
    w_ref, feat_ref, cot_ref = refs[len(sources) : len(sources) + 3]
    outs = refs[len(sources) + 3 + chained :]
    layer_ref, part_ref, back_refs = outs[0], outs[1], outs[2:]
    weight = w_ref[0]
    tokens = feat_ref.shape[0]
    depth = weight.shape[0]
    part = None
    for begin in range(0, tokens, tile):
        span = slice(begin, begin + tile)
        first = jnp.concatenate(
            [
                ref[:, unit, 0, :, span].astype(jnp.float32)
                for ref, units in zip(r_refs, sources)
                for unit in range(units)
            ],
            axis=1,
        )
        first = first.reshape(depth, tile).astype(jnp.bfloat16)
        value = contract(first, weight, 0, 0)
        square = value * value
        tangent = jnp.tanh(GELU_SCALE * (value + 0.044715 * square * value))
        half = 0.5 * (1.0 + tangent)
        layer_ref[span, :] = (feat_ref[span, :].astype(jnp.float32) + value * half).astype(
            jnp.bfloat16
        )
        rate = half + 0.5 * value * (1.0 - tangent * tangent) * GELU_SCALE * (
            1.0 + 3.0 * 0.044715 * square
        )
        slope = (cot_ref[span, :].astype(jnp.float32) * rate).astype(jnp.bfloat16)
        back = contract(weight, slope, 1, 1).reshape(owners, depth // owners, tile)
        start = 0
        for units, back_ref in zip(backs, back_refs):
            for unit in range(units):
                back_ref[:, unit, 0, :, span] = back[:, start : start + group].astype(jnp.bfloat16)
                start += group
        term = contract(first, slope, 1, 0)
        part = term if part is None else part + term
    part_ref[0] = part.astype(jnp.bfloat16)


def middle_part(received, w_two, features, cotangent, layer, low, high, backs):
    tokens, columns = features.shape
    owners, _, _, group, _ = received[0][0].shape
    count = high - low
    depth, width = w_two.shape[1:]
    tile = min(256, tokens)
    chained = 0 if layer is None else 1
    column = pl.BlockSpec((tokens, width), lambda j: (0, low + j))
    sources = [array.shape[1] for array, _ in received]
    operands = [array for array, _ in received] + [w_two, features, cotangent]
    operands += [layer] if chained else []

    def spec(units, skipped):
        return pl.BlockSpec(
            (owners, units, 1, group, tokens), lambda j: (0, 0, low - skipped + j, 0, 0)
        )

    return pl.pallas_call(
        functools.partial(middle_kernel, owners, group, sources, backs, tile, chained),
        grid=(count,),
        in_specs=[spec(array.shape[1], skipped) for array, skipped in received]
        + [pl.BlockSpec((1, depth, width), lambda j: (low + j, 0, 0)), column, column]
        + [pl.BlockSpec(memory_space=pl.ANY)] * chained,
        out_specs=[column, pl.BlockSpec((1, depth, width), lambda j: (j, 0, 0))]
        + [spec(units, low) for units in backs],
        out_shape=[
            jax.ShapeDtypeStruct((tokens, columns), jnp.bfloat16),
            jax.ShapeDtypeStruct((count, depth, width), jnp.bfloat16),
        ]
        + [
            jax.ShapeDtypeStruct((owners, units, count, group, tokens), jnp.bfloat16)
            for units in backs
        ],
        input_output_aliases={len(operands) - 1: 0} if chained else {},
        compiler_params=pltpu.CompilerParams(vmem_limit_bytes=VMEM_LIMIT),
        cost_estimate=pl.CostEstimate(
            flops=6 * count * tokens * depth * width,
            bytes_accessed=count * (10 * tokens * width + 4 * depth * width),
            transcendentals=count * tokens * width,
        ),
        name="middle",
    )(*operands)


def last_kernel(held, sources, shares, chained, *refs):
    q_refs = refs[: len(sources)]
    w_ref, feat_ref, cot_ref = refs[len(sources) : len(sources) + 3]
    grad_ref, part_ref, swap, total = refs[len(sources) + 3 + chained :]
    group, width, _ = w_ref.shape
    tokens = feat_ref.shape[0]
    lanes = tokens // LANES
    step = pl.program_id(0)

    @pl.when(step == 0)
    def _():
        total[...] = jnp.zeros_like(total)

    for q_ref, (low, high) in zip(q_refs, sources):
        for owner in range(q_ref.shape[0]):
            start = (owner * held + low) * group
            for lane in range(lanes):
                block = q_ref[owner, 0, :, :, lane * LANES : (lane + 1) * LANES]
                swap[lane, pl.ds(start, (high - low) * group), :] = block.astype(
                    jnp.float32
                ).reshape((high - low) * group, LANES)
    for b in range(group):
        back = jnp.concatenate(
            [swap[lane, pl.ds(b, width, stride=group), :] for lane in range(lanes)], axis=1
        ).astype(jnp.bfloat16)
        columns = slice(b * width, (b + 1) * width)
        through = contract(back, w_ref[b], 0, 1)
        grad_ref[:, columns] = (cot_ref[:, columns].astype(jnp.float32) + through).astype(
            jnp.bfloat16
        )
        total[b] += contract(back, feat_ref[:, columns], 1, 0)

    @pl.when(step == pl.num_programs(0) - 1)
    def _():
        rows = width // shares
        for b in range(group):
            part = total[b].T.astype(jnp.bfloat16)
            for share in range(shares):
                part_ref[share, b] = part[share * rows : (share + 1) * rows]


def last_part(returned, unit, w_one, features, cotangent, grad, shares):
    tokens, columns = features.shape
    width = w_one.shape[1]
    owners, _, _, group, _ = returned[0][0].shape
    tile = min(256, tokens)
    chained = 0 if grad is None else 1
    strip = pl.BlockSpec((tile, group * width), lambda t: (t, unit))
    operands = [array for array, _ in returned] + [w_one, features, cotangent]
    operands += [grad] if chained else []
    specs, sources, held = [], [], 0
    for array, at in returned:
        count = array.shape[2]
        index_map = functools.partial(lambda at, t: (0, at, 0, 0, t), at)
        specs.append(pl.BlockSpec((owners, 1, count, group, tile), index_map))
        sources.append((held, held + count))
        held += count
    return pl.pallas_call(
        functools.partial(last_kernel, held, sources, shares, chained),
        grid=(tokens // tile,),
        in_specs=specs
        + [pl.BlockSpec((group, width, width), lambda t: (unit, 0, 0)), strip, strip]
        + [pl.BlockSpec(memory_space=pl.ANY)] * chained,
        out_specs=[
            strip,
            pl.BlockSpec((shares, group, width // shares, width), lambda t: (0, 0, 0, 0)),
        ],
        out_shape=[
            jax.ShapeDtypeStruct((tokens, columns), jnp.bfloat16),
            jax.ShapeDtypeStruct((shares, group, width // shares, width), jnp.bfloat16),
        ],
        input_output_aliases={len(operands) - 1: 0} if chained else {},
        scratch_shapes=[
            pltpu.VMEM((tile // LANES, width * group, LANES), jnp.float32),
            pltpu.VMEM((group, width, width), jnp.float32),
        ],
        compiler_params=pltpu.CompilerParams(vmem_limit_bytes=VMEM_LIMIT),
        cost_estimate=pl.CostEstimate(
            flops=4 * group * tokens * width * width,
            bytes_accessed=group * (8 * tokens * width + 4 * width * width),
            transcendentals=0,
        ),
        name="last",
    )(*operands)


def exchange(array, before=None):
    if before is not None:
        array = after(array, before)
    return lax.all_to_all(array, "mp", split_axis=0, concat_axis=0, tiled=True)


def after(array, before):
    return lax.optimization_barrier((array, before))[0]


def swap_with(array, step):
    size = lax.axis_size("dp")
    return lax.ppermute(array, "dp", [(d, d ^ step) for d in range(size)])


def gathered_parts(part):
    parts = [part]
    step = lax.axis_size("dp") // 2
    while step:
        came = [swap_with(array, step) for array in parts]
        parts = [array for pair in zip(parts, came) for array in pair]
        step //= 2
    return parts


def scattered_terms(parts):
    me = lax.axis_index("dp")
    take = lambda step: lax.dynamic_index_in_dim(parts, me ^ step, 0, keepdims=False)
    return [take(0)] + [swap_with(take(step), step) for step in range(1, parts.shape[0])]


def scatter(part):
    return lax.psum_scatter(part, "dp", scatter_dimension=1, tiled=True)


def on_device(features, cotangent, factor_one, factor_two):
    owners = lax.axis_size("mp")
    shares = lax.axis_size("dp")
    held = factor_one.shape[0]
    half = held // 2
    unit = 8 if held % 16 == 0 else held
    units = held // unit

    position = jnp.full((1,), lax.axis_index("dp"), jnp.int32)
    parts = gathered_parts(factor_one[:unit])
    (head,) = first_head(position, features, parts, [(0, held)], owners, held)
    w_one = lax.all_gather(after(factor_one, head), "dp", axis=1, tiled=True)
    w_two = lax.all_gather(after(factor_two, w_one), "dp", axis=1, tiled=True)
    latest = arrived = exchange(head)
    received = [[(arrived, 0)], [(arrived, 0)]]
    if units > 1:
        cuts = [(0, half), (half, held)]
        rest = first_parts(
            after(features, head), w_one, unit, cuts, owners, held, 1, units - 1
        )
        for index, array in enumerate(rest):
            latest = exchange(array, latest)
            received[index].append((latest, index * half))

    backs = [units - 1, 1] if units > 1 else [1]
    layer, part_low, back_low = middle_part(
        received[0], w_two, features, cotangent, None, 0, half, [units]
    )
    latest = back_low = exchange(back_low, latest)
    layer, part_high, *back_high = middle_part(
        received[1], w_two, features, cotangent, layer, half, held, backs
    )
    for index, array in enumerate(back_high):
        latest = back_high[index] = exchange(array, latest)
    parts_two = [scatter(part_low), scatter(part_high)]

    grad, parts_one = None, []
    for index in range(units):
        if units > 1 and index == units - 1:
            back, at = after(back_high[1], parts_one), 0
        else:
            back, at = back_high[0], index
        grad, part = last_part(
            [(back_low, index), (back, at)], index, w_one, features, cotangent, grad, shares
        )
        terms = [term.astype(jnp.float32) for term in scattered_terms(part)]
        parts_one.append(sum(terms[1:], terms[0]))
    return (
        layer,
        grad,
        jnp.concatenate(parts_one, axis=0),
        jnp.concatenate(parts_two, axis=0).astype(jnp.float32),
    )


def solution(mesh):
    in_specs = (P("dp", "mp"), P("dp", "mp"), P("mp", "dp", None), P("mp", "dp", None))
    out_specs = (P("dp", "mp"), P("dp", "mp"), P("mp", "dp", None), P("mp", "dp", None))
    return jax.shard_map(
        on_device, mesh=mesh, in_specs=in_specs, out_specs=out_specs, check_vma=False
    )
```

```python
import functools
import math

import jax
import jax.numpy as jnp
from jax import lax
from jax.experimental import pallas as pl
from jax.experimental.pallas import tpu as pltpu
from jax.sharding import PartitionSpec as P

LANES = 128
VMEM_LIMIT = 60 * 1024 * 1024
GELU_SCALE = math.sqrt(2.0 / math.pi)


def contract(left, right, left_axis, right_axis):
    return lax.dot_general(
        left, right, (((left_axis,), (right_axis,)), ((), ())), preferred_element_type=jnp.float32
    )


def first_rows(feat_ref, weight, out_refs, unit, cuts, owners, held, swap):
    tokens = feat_ref.shape[0]
    group, width, _ = weight.shape
    for b in range(group):
        rows = contract(weight[b], feat_ref[:, b * width : (b + 1) * width], 1, 1)
        for lane in range(tokens // LANES):
            swap[lane, pl.ds(b, width, stride=group), :] = rows[
                :, lane * LANES : (lane + 1) * LANES
            ]
    for out_ref, (low, high) in zip(out_refs, cuts):
        for owner in range(owners):
            start = (owner * held + low) * group
            for lane in range(tokens // LANES):
                block = swap[lane, pl.ds(start, (high - low) * group), :]
                out_ref[owner, unit, :, :, lane * LANES : (lane + 1) * LANES] = block.reshape(
                    high - low, group, LANES
                ).astype(jnp.bfloat16)


def first_kernel(cuts, owners, held, units, *refs):
    feat_refs, w_refs, out_refs = refs[:units], refs[units : 2 * units], refs[2 * units : -2]
    weight, swap = refs[-2:]

    @pl.when(pl.program_id(0) == 0)
    def _():
        for unit, w_ref in enumerate(w_refs):
            for b in range(w_ref.shape[0]):
                weight[unit, b] = w_ref[b].T

    for unit in range(units):
        first_rows(feat_refs[unit], weight.at[unit], out_refs, unit, cuts, owners, held, swap)


def head_kernel(cuts, owners, held, shares, position_ref, feat_ref, *refs):
    part_refs, gathered, weight, swap = refs[:shares], *refs[-3:]
    rows = weight.shape[1] // shares

    @pl.when(pl.program_id(0) == 0)
    def _():
        for step, part_ref in enumerate(part_refs):
            start = pl.multiple_of((position_ref[0] ^ step) * rows, rows)
            gathered[:, pl.ds(start, rows), :] = part_ref[...]
        for b in range(weight.shape[0]):
            weight[b] = gathered[b].T

    first_rows(feat_ref, weight, refs[shares:-3], 0, cuts, owners, held, swap)


def first_call(features, group, width, cuts, owners, begin, units):
    tokens = features.shape[0]
    tile = min(256, tokens)
    outs = [
        jax.ShapeDtypeStruct((owners, units, high - low, group, tokens), jnp.bfloat16)
        for low, high in cuts
    ]
    moved = 2 * units * (tokens * group * width + group * width * width)
    moved += sum(2 * math.prod(out.shape) for out in outs)
    feat_specs = [
        pl.BlockSpec((tile, group * width), functools.partial(lambda u, t, *_: (t, u), begin + u))
        for u in range(units)
    ]
    out_specs = [
        pl.BlockSpec((owners, units, high - low, group, tile), lambda t, *_: (0, 0, 0, 0, t))
        for low, high in cuts
    ]
    swap = pltpu.VMEM((tile // LANES, width * group, LANES), jnp.float32)
    params = dict(
        out_shape=outs,
        compiler_params=pltpu.CompilerParams(vmem_limit_bytes=VMEM_LIMIT),
        cost_estimate=pl.CostEstimate(
            flops=2 * units * tokens * group * width * width,
            bytes_accessed=moved,
            transcendentals=0,
        ),
        name="first",
    )
    return (tokens // tile,), feat_specs, out_specs, swap, params


def first_parts(features, w_one, group, cuts, owners, held, begin, units):
    width = w_one.shape[1]
    grid, feat_specs, out_specs, swap, params = first_call(
        features, group, width, cuts, owners, begin, units
    )
    w_specs = [
        pl.BlockSpec((group, width, width), functools.partial(lambda u, t: (u, 0, 0), begin + u))
        for u in range(units)
    ]
    return pl.pallas_call(
        functools.partial(first_kernel, cuts, owners, held, units),
        grid=grid,
        in_specs=feat_specs + w_specs,
        out_specs=out_specs,
        scratch_shapes=[pltpu.VMEM((units, group, width, width), jnp.bfloat16), swap],
        **params,
    )(*[features] * units, *[w_one] * units)


def first_head(position, features, parts, cuts, owners, held):
    group, rows, width = parts[0].shape
    shares = len(parts)
    grid, feat_specs, out_specs, swap, params = first_call(
        features, group, width, cuts, owners, 0, 1
    )
    return pl.pallas_call(
        functools.partial(head_kernel, cuts, owners, held, shares),
        grid_spec=pltpu.PrefetchScalarGridSpec(
            num_scalar_prefetch=1,
            grid=grid,
            in_specs=feat_specs
            + [pl.BlockSpec((group, rows, width), lambda t, _: (0, 0, 0))] * shares,
            out_specs=out_specs,
            scratch_shapes=[pltpu.VMEM((group, width, width), jnp.bfloat16)] * 2 + [swap],
        ),
        **params,
    )(position, features, *parts)


def middle_kernel(owners, group, sources, backs, tile, chained, *refs):
    r_refs = refs[: len(sources)]
    w_ref, feat_ref, cot_ref = refs[len(sources) : len(sources) + 3]
    outs = refs[len(sources) + 3 + chained :]
    layer_ref, part_ref, back_refs = outs[0], outs[1], outs[2:]
    weight = w_ref[0]
    tokens = feat_ref.shape[0]
    depth = weight.shape[0]
    part = None
    for begin in range(0, tokens, tile):
        span = slice(begin, begin + tile)
        first = jnp.concatenate(
            [
                ref[:, unit, 0, :, span].astype(jnp.float32)
                for ref, units in zip(r_refs, sources)
                for unit in range(units)
            ],
            axis=1,
        )
        first = first.reshape(depth, tile).astype(jnp.bfloat16)
        value = contract(first, weight, 0, 0)
        square = value * value
        tangent = jnp.tanh(GELU_SCALE * (value + 0.044715 * square * value))
        half = 0.5 * (1.0 + tangent)
        layer_ref[span, :] = (feat_ref[span, :].astype(jnp.float32) + value * half).astype(
            jnp.bfloat16
        )
        rate = half + 0.5 * value * (1.0 - tangent * tangent) * GELU_SCALE * (
            1.0 + 3.0 * 0.044715 * square
        )
        slope = (cot_ref[span, :].astype(jnp.float32) * rate).astype(jnp.bfloat16)
        back = contract(weight, slope, 1, 1).reshape(owners, depth // owners, tile)
        start = 0
        for units, back_ref in zip(backs, back_refs):
            for unit in range(units):
                back_ref[:, unit, 0, :, span] = back[:, start : start + group].astype(jnp.bfloat16)
                start += group
        term = contract(first, slope, 1, 0)
        part = term if part is None else part + term
    part_ref[0] = part.astype(jnp.bfloat16)


def middle_part(received, w_two, features, cotangent, layer, low, high, backs):
    tokens, columns = features.shape
    owners, _, _, group, _ = received[0][0].shape
    count = high - low
    depth, width = w_two.shape[1:]
    tile = min(256, tokens)
    chained = 0 if layer is None else 1
    column = pl.BlockSpec((tokens, width), lambda j: (0, low + j))
    sources = [array.shape[1] for array, _ in received]
    operands = [array for array, _ in received] + [w_two, features, cotangent]
    operands += [layer] if chained else []

    def spec(units, skipped):
        return pl.BlockSpec(
            (owners, units, 1, group, tokens), lambda j: (0, 0, low - skipped + j, 0, 0)
        )

    return pl.pallas_call(
        functools.partial(middle_kernel, owners, group, sources, backs, tile, chained),
        grid=(count,),
        in_specs=[spec(array.shape[1], skipped) for array, skipped in received]
        + [pl.BlockSpec((1, depth, width), lambda j: (low + j, 0, 0)), column, column]
        + [pl.BlockSpec(memory_space=pl.ANY)] * chained,
        out_specs=[column, pl.BlockSpec((1, depth, width), lambda j: (j, 0, 0))]
        + [spec(units, low) for units in backs],
        out_shape=[
            jax.ShapeDtypeStruct((tokens, columns), jnp.bfloat16),
            jax.ShapeDtypeStruct((count, depth, width), jnp.bfloat16),
        ]
        + [
            jax.ShapeDtypeStruct((owners, units, count, group, tokens), jnp.bfloat16)
            for units in backs
        ],
        input_output_aliases={len(operands) - 1: 0} if chained else {},
        compiler_params=pltpu.CompilerParams(vmem_limit_bytes=VMEM_LIMIT),
        cost_estimate=pl.CostEstimate(
            flops=6 * count * tokens * depth * width,
            bytes_accessed=count * (10 * tokens * width + 4 * depth * width),
            transcendentals=count * tokens * width,
        ),
        name="middle",
    )(*operands)


def last_kernel(held, sources, shares, rows_out, grad_out, chained, position_ref, *refs):
    q_refs, refs = refs[: len(sources)], list(refs[len(sources) :])
    feat_ref = refs.pop(0) if rows_out else None
    w_ref, cot_ref = (refs.pop(0), refs.pop(0)) if grad_out else (None, None)
    refs = refs[chained:]
    keep_ref, send_ref = (refs.pop(0), refs.pop(0)) if rows_out else (None, None)
    grad_ref = refs.pop(0) if grad_out else None
    swap = refs.pop(0)
    total = refs.pop(0) if rows_out else None
    group, tokens = q_refs[0].shape[3:]
    width = swap.shape[1] // group
    lanes = tokens // LANES
    step = pl.program_id(0)

    if rows_out:

        @pl.when(step == 0)
        def _():
            total[...] = jnp.zeros_like(total)

    for q_ref, (low, high) in zip(q_refs, sources):
        for owner in range(q_ref.shape[0]):
            start = (owner * held + low) * group
            for lane in range(lanes):
                block = q_ref[owner, 0, :, :, lane * LANES : (lane + 1) * LANES]
                swap[lane, pl.ds(start, (high - low) * group), :] = block.astype(
                    jnp.float32
                ).reshape((high - low) * group, LANES)
    for b in range(group):
        back = jnp.concatenate(
            [swap[lane, pl.ds(b, width, stride=group), :] for lane in range(lanes)], axis=1
        ).astype(jnp.bfloat16)
        columns = slice(b * width, (b + 1) * width)
        if grad_out:
            through = contract(back, w_ref[b], 0, 1)
            grad_ref[:, columns] = (cot_ref[:, columns].astype(jnp.float32) + through).astype(
                jnp.bfloat16
            )
        if rows_out:
            total[b] += contract(back, feat_ref[:, columns], 1, 0)

    if rows_out:

        @pl.when(step == pl.num_programs(0) - 1)
        def _():
            rows = width // shares
            me = position_ref[0]
            for b in range(group):
                part = total[b].T.astype(jnp.bfloat16)
                for share in range(shares):
                    mine = (me & 1) == (share & 1)
                    place = (me >> 1) ^ (share >> 1)
                    block = part[share * rows : (share + 1) * rows]

                    @pl.when(mine)
                    def _():
                        keep_ref[place, b] = block

                    @pl.when(jnp.logical_not(mine))
                    def _():
                        send_ref[place, b] = block


def last_part(position, returned, unit, rows_of, grad_of, grad, shares):
    tokens = returned[0][0].shape[-1]
    owners, _, _, group, _ = returned[0][0].shape
    held = sum(array.shape[2] for array, _ in returned)
    width = owners * held
    tile = min(256, tokens)
    strip = pl.BlockSpec((tile, group * width), lambda t, _: (t, unit))
    operands, specs, sources, low = [], [], [], 0
    for array, at in returned:
        count = array.shape[2]
        index_map = functools.partial(lambda at, t, _: (0, at, 0, 0, t), at)
        operands.append(array)
        specs.append(pl.BlockSpec((owners, 1, count, group, tile), index_map))
        sources.append((low, low + count))
        low += count
    outs, out_specs, aliases = [], [], {}
    scratch = [pltpu.VMEM((tile // LANES, width * group, LANES), jnp.float32)]
    chained = 1 if grad_of is not None and grad is not None else 0
    if rows_of is not None:
        operands.append(rows_of)
        specs.append(strip)
        block = (shares // 2, group, width // shares, width)
        outs += [jax.ShapeDtypeStruct(block, jnp.bfloat16)] * 2
        out_specs += [pl.BlockSpec(block, lambda t, _: (0, 0, 0, 0))] * 2
        scratch.append(pltpu.VMEM((group, width, width), jnp.float32))
    if grad_of is not None:
        w_one, cotangent = grad_of
        operands += [w_one, cotangent]
        specs += [pl.BlockSpec((group, width, width), lambda t, _: (unit, 0, 0)), strip]
        if chained:
            operands.append(grad)
            specs.append(pl.BlockSpec(memory_space=pl.ANY))
            aliases = {len(operands): len(outs)}
        outs.append(jax.ShapeDtypeStruct(cotangent.shape, jnp.bfloat16))
        out_specs.append(strip)
    jobs = (rows_of is not None) + (grad_of is not None)
    return pl.pallas_call(
        functools.partial(
            last_kernel, held, sources, shares, rows_of is not None, grad_of is not None, chained
        ),
        grid_spec=pltpu.PrefetchScalarGridSpec(
            num_scalar_prefetch=1,
            grid=(tokens // tile,),
            in_specs=specs,
            out_specs=out_specs,
            scratch_shapes=scratch,
        ),
        out_shape=outs,
        input_output_aliases=aliases,
        compiler_params=pltpu.CompilerParams(vmem_limit_bytes=VMEM_LIMIT),
        cost_estimate=pl.CostEstimate(
            flops=2 * jobs * group * tokens * width * width,
            bytes_accessed=group * (2 + 3 * jobs) * tokens * width,
            transcendentals=0,
        ),
        name="last",
    )(position, *operands)


def exchange(array, before=None):
    if before is not None:
        array = after(array, before)
    return lax.all_to_all(array, "mp", split_axis=0, concat_axis=0, tiled=True)


def after(array, before):
    return lax.optimization_barrier((array, before))[0]


def swap_with(array, step):
    size = lax.axis_size("dp")
    return lax.ppermute(array, "dp", [(d, d ^ step) for d in range(size)])


def gathered_parts(part):
    parts = [part]
    step = lax.axis_size("dp") // 2
    while step:
        came = [swap_with(array, step) for array in parts]
        parts = [array for pair in zip(parts, came) for array in pair]
        step //= 2
    return parts


def summed(keep, send):
    total = keep.astype(jnp.float32) + swap_with(send, 1).astype(jnp.float32)
    count = total.shape[0]
    leaving = []
    while count > 1:
        count //= 2
        leaving.append(total[count:].astype(jnp.bfloat16))
        came = swap_with(leaving[-1], 2 * count)
        total = total[:count] + came.astype(jnp.float32)
    return total[0], leaving


def scatter(part):
    return lax.psum_scatter(part, "dp", scatter_dimension=1, tiled=True)


def on_device(features, cotangent, factor_one, factor_two):
    owners = lax.axis_size("mp")
    shares = lax.axis_size("dp")
    held = factor_one.shape[0]
    half = held // 2
    unit = 8 if held % 16 == 0 else held
    units = held // unit

    position = jnp.full((1,), lax.axis_index("dp"), jnp.int32)
    parts = gathered_parts(factor_one[:unit])
    (head,) = first_head(position, features, parts, [(0, held)], owners, held)
    w_one = lax.all_gather(after(factor_one, head), "dp", axis=1, tiled=True)
    w_two = lax.all_gather(after(factor_two, w_one), "dp", axis=1, tiled=True)
    latest = arrived = exchange(head)
    received = [[(arrived, 0)], [(arrived, 0)]]
    if units > 1:
        cuts = [(0, half), (half, held)]
        rest = first_parts(
            after(features, head), w_one, unit, cuts, owners, held, 1, units - 1
        )
        for index, array in enumerate(rest):
            latest = exchange(array, latest)
            received[index].append((latest, index * half))

    backs = [units - 1, 1] if units > 1 else [1]
    layer, part_low, back_low = middle_part(
        received[0], w_two, features, cotangent, None, 0, half, [units]
    )
    latest = back_low = exchange(back_low, latest)
    layer, part_high, *back_high = middle_part(
        received[1], w_two, features, cotangent, layer, half, held, backs
    )
    for index, array in enumerate(back_high):
        latest = back_high[index] = exchange(array, latest)
    parts_two = [scatter(part_low), scatter(part_high)]

    grad, hops, parts_one = None, [], []
    for index in range(units):
        final = units > 1 and index == units - 1
        back, at = (back_high[1], 0) if final else (back_high[0], index)
        if index:
            back = after(back, (hops, parts_one[:-1]))
        returned = [(back_low, index), (back, at)]
        grad_of = (w_one, cotangent)
        if final:
            keep, send = last_part(position, returned, index, features, None, None, shares)
            (grad,) = last_part(position, returned, index, None, grad_of, grad, shares)
        else:
            keep, send, grad = last_part(
                position, returned, index, features, grad_of, grad, shares
            )
        part, hops = summed(keep, send)
        parts_one.append(part)
    grad_one = jnp.concatenate(
        parts_one[:-1] + [jnp.zeros_like(parts_one[-1])], axis=0
    )
    grad_one = lax.dynamic_update_slice(grad_one, parts_one[-1], (held - unit, 0, 0))
    return (
        layer,
        grad,
        grad_one,
        jnp.concatenate(parts_two, axis=0).astype(jnp.float32),
    )


def solution(mesh):
    in_specs = (P("dp", "mp"), P("dp", "mp"), P("mp", "dp", None), P("mp", "dp", None))
    out_specs = (P("dp", "mp"), P("dp", "mp"), P("mp", "dp", None), P("mp", "dp", None))
    return jax.shard_map(
        on_device, mesh=mesh, in_specs=in_specs, out_specs=out_specs, check_vma=False
    )
```

```python
import functools
import math

import jax
import jax.numpy as jnp
from jax import lax
from jax.experimental import pallas as pl
from jax.experimental.pallas import tpu as pltpu
from jax.sharding import PartitionSpec as P

LANES = 128
VMEM_LIMIT = 60 * 1024 * 1024
GELU_SCALE = math.sqrt(2.0 / math.pi)


def contract(left, right, left_axis, right_axis):
    return lax.dot_general(
        left, right, (((left_axis,), (right_axis,)), ((), ())), preferred_element_type=jnp.float32
    )


def first_rows(feat_ref, weight, out_refs, unit, cuts, owners, held, swap):
    tokens = feat_ref.shape[0]
    group, width, _ = weight.shape
    for b in range(group):
        rows = contract(weight[b], feat_ref[:, b * width : (b + 1) * width], 1, 1)
        for lane in range(tokens // LANES):
            swap[lane, pl.ds(b, width, stride=group), :] = rows[
                :, lane * LANES : (lane + 1) * LANES
            ]
    for out_ref, (low, high) in zip(out_refs, cuts):
        for owner in range(owners):
            start = (owner * held + low) * group
            for lane in range(tokens // LANES):
                block = swap[lane, pl.ds(start, (high - low) * group), :]
                out_ref[owner, unit, :, :, lane * LANES : (lane + 1) * LANES] = block.reshape(
                    high - low, group, LANES
                ).astype(jnp.bfloat16)


def first_kernel(cuts, owners, held, units, *refs):
    feat_refs, w_refs, out_refs = refs[:units], refs[units : 2 * units], refs[2 * units : -2]
    weight, swap = refs[-2:]

    @pl.when(pl.program_id(0) == 0)
    def _():
        for unit, w_ref in enumerate(w_refs):
            for b in range(w_ref.shape[0]):
                weight[unit, b] = w_ref[b].T

    for unit in range(units):
        first_rows(feat_refs[unit], weight.at[unit], out_refs, unit, cuts, owners, held, swap)


def head_kernel(cuts, owners, held, shares, position_ref, feat_ref, *refs):
    part_refs, gathered, weight, swap = refs[:shares], *refs[-3:]
    rows = weight.shape[1] // shares

    @pl.when(pl.program_id(0) == 0)
    def _():
        for step, part_ref in enumerate(part_refs):
            start = pl.multiple_of((position_ref[0] ^ step) * rows, rows)
            gathered[:, pl.ds(start, rows), :] = part_ref[...]
        for b in range(weight.shape[0]):
            weight[b] = gathered[b].T

    first_rows(feat_ref, weight, refs[shares:-3], 0, cuts, owners, held, swap)


def first_call(features, group, width, cuts, owners, begin, units):
    tokens = features.shape[0]
    tile = min(256, tokens)
    outs = [
        jax.ShapeDtypeStruct((owners, units, high - low, group, tokens), jnp.bfloat16)
        for low, high in cuts
    ]
    moved = 2 * units * (tokens * group * width + group * width * width)
    moved += sum(2 * math.prod(out.shape) for out in outs)
    feat_specs = [
        pl.BlockSpec((tile, group * width), functools.partial(lambda u, t, *_: (t, u), begin + u))
        for u in range(units)
    ]
    out_specs = [
        pl.BlockSpec((owners, units, high - low, group, tile), lambda t, *_: (0, 0, 0, 0, t))
        for low, high in cuts
    ]
    swap = pltpu.VMEM((tile // LANES, width * group, LANES), jnp.float32)
    params = dict(
        out_shape=outs,
        compiler_params=pltpu.CompilerParams(vmem_limit_bytes=VMEM_LIMIT),
        cost_estimate=pl.CostEstimate(
            flops=2 * units * tokens * group * width * width,
            bytes_accessed=moved,
            transcendentals=0,
        ),
        name="first",
    )
    return (tokens // tile,), feat_specs, out_specs, swap, params


def first_parts(features, w_one, group, cuts, owners, held, begin, units):
    width = w_one.shape[1]
    grid, feat_specs, out_specs, swap, params = first_call(
        features, group, width, cuts, owners, begin, units
    )
    w_specs = [
        pl.BlockSpec((group, width, width), functools.partial(lambda u, t: (u, 0, 0), begin + u))
        for u in range(units)
    ]
    return pl.pallas_call(
        functools.partial(first_kernel, cuts, owners, held, units),
        grid=grid,
        in_specs=feat_specs + w_specs,
        out_specs=out_specs,
        scratch_shapes=[pltpu.VMEM((units, group, width, width), jnp.bfloat16), swap],
        **params,
    )(*[features] * units, *[w_one] * units)


def first_head(position, features, parts, cuts, owners, held):
    group, rows, width = parts[0].shape
    shares = len(parts)
    grid, feat_specs, out_specs, swap, params = first_call(
        features, group, width, cuts, owners, 0, 1
    )
    return pl.pallas_call(
        functools.partial(head_kernel, cuts, owners, held, shares),
        grid_spec=pltpu.PrefetchScalarGridSpec(
            num_scalar_prefetch=1,
            grid=grid,
            in_specs=feat_specs
            + [pl.BlockSpec((group, rows, width), lambda t, _: (0, 0, 0))] * shares,
            out_specs=out_specs,
            scratch_shapes=[pltpu.VMEM((group, width, width), jnp.bfloat16)] * 2 + [swap],
        ),
        **params,
    )(position, features, *parts)


def middle_kernel(owners, group, sources, backs, tile, chained, *refs):
    r_refs = refs[: len(sources)]
    w_ref, feat_ref, cot_ref = refs[len(sources) : len(sources) + 3]
    outs = refs[len(sources) + 3 + chained :]
    layer_ref, part_ref, back_refs = outs[0], outs[1], outs[2:]
    weight = w_ref[0]
    tokens = feat_ref.shape[0]
    depth = weight.shape[0]
    part = None
    for begin in range(0, tokens, tile):
        span = slice(begin, begin + tile)
        first = jnp.concatenate(
            [
                ref[:, unit, 0, :, span].astype(jnp.float32)
                for ref, units in zip(r_refs, sources)
                for unit in range(units)
            ],
            axis=1,
        )
        first = first.reshape(depth, tile).astype(jnp.bfloat16)
        value = contract(first, weight, 0, 0)
        square = value * value
        tangent = jnp.tanh(GELU_SCALE * (value + 0.044715 * square * value))
        half = 0.5 * (1.0 + tangent)
        layer_ref[span, :] = (feat_ref[span, :].astype(jnp.float32) + value * half).astype(
            jnp.bfloat16
        )
        rate = half + 0.5 * value * (1.0 - tangent * tangent) * GELU_SCALE * (
            1.0 + 3.0 * 0.044715 * square
        )
        slope = (cot_ref[span, :].astype(jnp.float32) * rate).astype(jnp.bfloat16)
        back = contract(weight, slope, 1, 1).reshape(owners, depth // owners, tile)
        start = 0
        for units, back_ref in zip(backs, back_refs):
            for unit in range(units):
                back_ref[:, unit, 0, :, span] = back[:, start : start + group].astype(jnp.bfloat16)
                start += group
        term = contract(first, slope, 1, 0)
        part = term if part is None else part + term
    part_ref[0] = part.astype(jnp.bfloat16)


def middle_part(received, w_two, features, cotangent, layer, low, high, backs):
    tokens, columns = features.shape
    owners, _, _, group, _ = received[0][0].shape
    count = high - low
    depth, width = w_two.shape[1:]
    tile = min(256, tokens)
    chained = 0 if layer is None else 1
    column = pl.BlockSpec((tokens, width), lambda j: (0, low + j))
    sources = [array.shape[1] for array, _ in received]
    operands = [array for array, _ in received] + [w_two, features, cotangent]
    operands += [layer] if chained else []

    def spec(units, skipped):
        return pl.BlockSpec(
            (owners, units, 1, group, tokens), lambda j: (0, 0, low - skipped + j, 0, 0)
        )

    return pl.pallas_call(
        functools.partial(middle_kernel, owners, group, sources, backs, tile, chained),
        grid=(count,),
        in_specs=[spec(array.shape[1], skipped) for array, skipped in received]
        + [pl.BlockSpec((1, depth, width), lambda j: (low + j, 0, 0)), column, column]
        + [pl.BlockSpec(memory_space=pl.ANY)] * chained,
        out_specs=[column, pl.BlockSpec((1, depth, width), lambda j: (j, 0, 0))]
        + [spec(units, low) for units in backs],
        out_shape=[
            jax.ShapeDtypeStruct((tokens, columns), jnp.bfloat16),
            jax.ShapeDtypeStruct((count, depth, width), jnp.bfloat16),
        ]
        + [
            jax.ShapeDtypeStruct((owners, units, count, group, tokens), jnp.bfloat16)
            for units in backs
        ],
        input_output_aliases={len(operands) - 1: 0} if chained else {},
        compiler_params=pltpu.CompilerParams(vmem_limit_bytes=VMEM_LIMIT),
        cost_estimate=pl.CostEstimate(
            flops=6 * count * tokens * depth * width,
            bytes_accessed=count * (10 * tokens * width + 4 * depth * width),
            transcendentals=count * tokens * width,
        ),
        name="middle",
    )(*operands)


def last_kernel(held, sources, shares, rows_out, grad_out, chained, position_ref, *refs):
    q_refs, refs = refs[: len(sources)], list(refs[len(sources) :])
    feat_ref = refs.pop(0) if rows_out else None
    w_ref, cot_ref = (refs.pop(0), refs.pop(0)) if grad_out else (None, None)
    refs = refs[chained:]
    keep_ref, send_ref = (refs.pop(0), refs.pop(0)) if rows_out else (None, None)
    grad_ref = refs.pop(0) if grad_out else None
    swap = refs.pop(0)
    total = refs.pop(0) if rows_out else None
    group, tokens = q_refs[0].shape[3:]
    width = swap.shape[1] // group
    lanes = tokens // LANES
    step = pl.program_id(0)

    if rows_out:

        @pl.when(step == 0)
        def _():
            total[...] = jnp.zeros_like(total)

    for q_ref, (low, high) in zip(q_refs, sources):
        for owner in range(q_ref.shape[0]):
            start = (owner * held + low) * group
            for lane in range(lanes):
                block = q_ref[owner, 0, :, :, lane * LANES : (lane + 1) * LANES]
                swap[lane, pl.ds(start, (high - low) * group), :] = block.astype(
                    jnp.float32
                ).reshape((high - low) * group, LANES)
    for b in range(group):
        back = jnp.concatenate(
            [swap[lane, pl.ds(b, width, stride=group), :] for lane in range(lanes)], axis=1
        ).astype(jnp.bfloat16)
        columns = slice(b * width, (b + 1) * width)
        if grad_out:
            through = contract(back, w_ref[b], 0, 1)
            grad_ref[:, columns] = (cot_ref[:, columns].astype(jnp.float32) + through).astype(
                jnp.bfloat16
            )
        if rows_out:
            total[b] += contract(back, feat_ref[:, columns], 1, 0)

    if rows_out:

        @pl.when(step == pl.num_programs(0) - 1)
        def _():
            rows = width // shares
            me = position_ref[0]
            for b in range(group):
                part = total[b].T.astype(jnp.bfloat16)
                for share in range(shares):
                    mine = (me & 1) == (share & 1)
                    place = (me >> 1) ^ (share >> 1)
                    block = part[share * rows : (share + 1) * rows]

                    @pl.when(mine)
                    def _():
                        keep_ref[place, b] = block

                    @pl.when(jnp.logical_not(mine))
                    def _():
                        send_ref[place, b] = block


def last_part(position, returned, unit, rows_of, grad_of, grad, shares):
    tokens = returned[0][0].shape[-1]
    owners, _, _, group, _ = returned[0][0].shape
    held = sum(array.shape[2] for array, _ in returned)
    width = owners * held
    tile = min(256, tokens)
    strip = pl.BlockSpec((tile, group * width), lambda t, _: (t, unit))
    operands, specs, sources, low = [], [], [], 0
    for array, at in returned:
        count = array.shape[2]
        index_map = functools.partial(lambda at, t, _: (0, at, 0, 0, t), at)
        operands.append(array)
        specs.append(pl.BlockSpec((owners, 1, count, group, tile), index_map))
        sources.append((low, low + count))
        low += count
    outs, out_specs, aliases = [], [], {}
    scratch = [pltpu.VMEM((tile // LANES, width * group, LANES), jnp.float32)]
    chained = 1 if grad_of is not None and grad is not None else 0
    if rows_of is not None:
        operands.append(rows_of)
        specs.append(strip)
        block = (shares // 2, group, width // shares, width)
        outs += [jax.ShapeDtypeStruct(block, jnp.bfloat16)] * 2
        out_specs += [pl.BlockSpec(block, lambda t, _: (0, 0, 0, 0))] * 2
        scratch.append(pltpu.VMEM((group, width, width), jnp.float32))
    if grad_of is not None:
        w_one, cotangent = grad_of
        operands += [w_one, cotangent]
        specs += [pl.BlockSpec((group, width, width), lambda t, _: (unit, 0, 0)), strip]
        if chained:
            operands.append(grad)
            specs.append(pl.BlockSpec(memory_space=pl.ANY))
            aliases = {len(operands): len(outs)}
        outs.append(jax.ShapeDtypeStruct(cotangent.shape, jnp.bfloat16))
        out_specs.append(strip)
    jobs = (rows_of is not None) + (grad_of is not None)
    return pl.pallas_call(
        functools.partial(
            last_kernel, held, sources, shares, rows_of is not None, grad_of is not None, chained
        ),
        grid_spec=pltpu.PrefetchScalarGridSpec(
            num_scalar_prefetch=1,
            grid=(tokens // tile,),
            in_specs=specs,
            out_specs=out_specs,
            scratch_shapes=scratch,
        ),
        out_shape=outs,
        input_output_aliases=aliases,
        compiler_params=pltpu.CompilerParams(vmem_limit_bytes=VMEM_LIMIT),
        cost_estimate=pl.CostEstimate(
            flops=2 * jobs * group * tokens * width * width,
            bytes_accessed=group * (2 + 3 * jobs) * tokens * width,
            transcendentals=0,
        ),
        name="last",
    )(position, *operands)


def exchange(array, before=None):
    if before is not None:
        array = after(array, before)
    return lax.all_to_all(array, "mp", split_axis=0, concat_axis=0, tiled=True)


def after(array, before):
    return lax.optimization_barrier((array, before))[0]


def swap_with(array, step):
    size = lax.axis_size("dp")
    return lax.ppermute(array, "dp", [(d, d ^ step) for d in range(size)])


def gathered_parts(part):
    parts = [part]
    step = lax.axis_size("dp") // 2
    while step:
        came = [swap_with(array, step) for array in parts]
        parts = [array for pair in zip(parts, came) for array in pair]
        step //= 2
    return parts


def first_hop(keep, send):
    return keep.astype(jnp.float32) + swap_with(send, 1).astype(jnp.float32)


def other_hops(totals):
    total = jnp.concatenate(totals, axis=1)
    count = total.shape[0]
    while count > 1:
        count //= 2
        came = swap_with(total[count:].astype(jnp.bfloat16), 2 * count)
        total = total[:count] + came.astype(jnp.float32)
    return total[0]


def scatter(part):
    return lax.psum_scatter(part, "dp", scatter_dimension=1, tiled=True)


def on_device(features, cotangent, factor_one, factor_two):
    owners = lax.axis_size("mp")
    shares = lax.axis_size("dp")
    held = factor_one.shape[0]
    half = held // 2
    unit = 8 if held % 16 == 0 else held
    units = held // unit

    position = jnp.full((1,), lax.axis_index("dp"), jnp.int32)
    parts = gathered_parts(factor_one[:unit])
    (head,) = first_head(position, features, parts, [(0, held)], owners, held)
    w_one = lax.all_gather(after(factor_one, head), "dp", axis=1, tiled=True)
    w_two = lax.all_gather(after(factor_two, w_one), "dp", axis=1, tiled=True)
    latest = arrived = exchange(head)
    received = [[(arrived, 0)], [(arrived, 0)]]
    if units > 1:
        cuts = [(0, half), (half, held)]
        rest = first_parts(
            after(features, head), w_one, unit, cuts, owners, held, 1, units - 1
        )
        for index, array in enumerate(rest):
            latest = exchange(array, latest)
            received[index].append((latest, index * half))

    backs = [units - 1, 1] if units > 1 else [1]
    layer, part_low, back_low = middle_part(
        received[0], w_two, features, cotangent, None, 0, half, [units]
    )
    latest = back_low = exchange(back_low, latest)
    layer, part_high, *back_high = middle_part(
        received[1], w_two, features, cotangent, layer, half, held, backs
    )
    parts_two = [scatter(part_low), scatter(part_high)]
    for index, array in enumerate(back_high):
        before = (latest, parts_two) if index else latest
        latest = back_high[index] = exchange(array, before)

    grad, hops, parts_one = None, [], []
    for index in range(units):
        final = units > 1 and index == units - 1
        back, at = (back_high[1], 0) if final else (back_high[0], index)
        if final:
            back = after(back, parts_one)
        returned = [(back_low, index), (back, at)]
        grad_of = (w_one, cotangent)
        if final:
            keep, send = last_part(position, returned, index, features, None, None, shares)
            (grad,) = last_part(position, returned, index, None, grad_of, grad, shares)
        else:
            keep, send, grad = last_part(
                position, returned, index, features, grad_of, grad, shares
            )
        hops.append(first_hop(keep, send))
        if index == units // 2 - 1 or index == units - 1:
            parts_one.append(other_hops(hops[-(units // 2 or 1) :]))
    parts_two = after(parts_two, hops[-1])
    grad_one = jnp.concatenate(parts_one[:-1] + [jnp.zeros_like(parts_one[-1])], axis=0)
    start = held - parts_one[-1].shape[0]
    grad_one = lax.dynamic_update_slice(grad_one, parts_one[-1], (start, 0, 0))
    return (
        layer,
        grad,
        grad_one,
        jnp.concatenate(parts_two, axis=0).astype(jnp.float32),
    )


def solution(mesh):
    in_specs = (P("dp", "mp"), P("dp", "mp"), P("mp", "dp", None), P("mp", "dp", None))
    out_specs = (P("dp", "mp"), P("dp", "mp"), P("mp", "dp", None), P("mp", "dp", None))
    return jax.shard_map(
        on_device, mesh=mesh, in_specs=in_specs, out_specs=out_specs, check_vma=False
    )
```

```python
import functools
import math

import jax
import jax.numpy as jnp
from jax import lax
from jax.experimental import pallas as pl
from jax.experimental.pallas import tpu as pltpu
from jax.sharding import PartitionSpec as P

LANES = 128
VMEM_LIMIT = 60 * 1024 * 1024
GELU_SCALE = math.sqrt(2.0 / math.pi)


def contract(left, right, left_axis, right_axis):
    return lax.dot_general(
        left, right, (((left_axis,), (right_axis,)), ((), ())), preferred_element_type=jnp.float32
    )


def first_rows(feat_ref, weight, out_refs, unit, cuts, owners, held, swap):
    tokens = feat_ref.shape[0]
    group, width, _ = weight.shape
    for b in range(group):
        rows = contract(weight[b], feat_ref[:, b * width : (b + 1) * width], 1, 1)
        for lane in range(tokens // LANES):
            swap[lane, pl.ds(b, width, stride=group + 1), :] = rows[
                :, lane * LANES : (lane + 1) * LANES
            ]
    for out_ref, (low, high) in zip(out_refs, cuts):
        for owner in range(owners):
            for j in range(low, high):
                start = (owner * held + j) * (group + 1)
                for lane in range(tokens // LANES):
                    block = swap[lane, pl.ds(start, group), :]
                    out_ref[owner, unit, j - low, :, lane * LANES : (lane + 1) * LANES] = (
                        block.astype(jnp.bfloat16)
                    )


def first_kernel(cuts, owners, held, units, *refs):
    feat_refs, w_refs, out_refs = refs[:units], refs[units : 2 * units], refs[2 * units : -2]
    weight, swap = refs[-2:]

    @pl.when(pl.program_id(0) == 0)
    def _():
        for unit, w_ref in enumerate(w_refs):
            for b in range(w_ref.shape[0]):
                weight[unit, b] = w_ref[b].T

    for unit in range(units):
        first_rows(feat_refs[unit], weight.at[unit], out_refs, unit, cuts, owners, held, swap)


def head_kernel(cuts, owners, held, shares, position_ref, feat_ref, *refs):
    part_refs, gathered, weight, swap = refs[:shares], *refs[-3:]
    rows = weight.shape[1] // shares

    @pl.when(pl.program_id(0) == 0)
    def _():
        for step, part_ref in enumerate(part_refs):
            start = pl.multiple_of((position_ref[0] ^ step) * rows, rows)
            gathered[:, pl.ds(start, rows), :] = part_ref[...]
        for b in range(weight.shape[0]):
            weight[b] = gathered[b].T

    first_rows(feat_ref, weight, refs[shares:-3], 0, cuts, owners, held, swap)


def first_call(features, group, width, cuts, owners, begin, units):
    tokens = features.shape[0]
    tile = min(256, tokens)
    outs = [
        jax.ShapeDtypeStruct((owners, units, high - low, group, tokens), jnp.bfloat16)
        for low, high in cuts
    ]
    moved = 2 * units * (tokens * group * width + group * width * width)
    moved += sum(2 * math.prod(out.shape) for out in outs)
    feat_specs = [
        pl.BlockSpec((tile, group * width), functools.partial(lambda u, t, *_: (t, u), begin + u))
        for u in range(units)
    ]
    out_specs = [
        pl.BlockSpec((owners, units, high - low, group, tile), lambda t, *_: (0, 0, 0, 0, t))
        for low, high in cuts
    ]
    swap = pltpu.VMEM((tile // LANES, width * (group + 1), LANES), jnp.float32)
    params = dict(
        out_shape=outs,
        compiler_params=pltpu.CompilerParams(vmem_limit_bytes=VMEM_LIMIT),
        cost_estimate=pl.CostEstimate(
            flops=2 * units * tokens * group * width * width,
            bytes_accessed=moved,
            transcendentals=0,
        ),
        name="first",
    )
    return (tokens // tile,), feat_specs, out_specs, swap, params


def first_parts(features, w_one, group, cuts, owners, held, begin, units):
    width = w_one.shape[1]
    grid, feat_specs, out_specs, swap, params = first_call(
        features, group, width, cuts, owners, begin, units
    )
    w_specs = [
        pl.BlockSpec((group, width, width), functools.partial(lambda u, t: (u, 0, 0), begin + u))
        for u in range(units)
    ]
    return pl.pallas_call(
        functools.partial(first_kernel, cuts, owners, held, units),
        grid=grid,
        in_specs=feat_specs + w_specs,
        out_specs=out_specs,
        scratch_shapes=[pltpu.VMEM((units, group, width, width), jnp.bfloat16), swap],
        **params,
    )(*[features] * units, *[w_one] * units)


def first_head(position, features, parts, cuts, owners, held):
    group, rows, width = parts[0].shape
    shares = len(parts)
    grid, feat_specs, out_specs, swap, params = first_call(
        features, group, width, cuts, owners, 0, 1
    )
    return pl.pallas_call(
        functools.partial(head_kernel, cuts, owners, held, shares),
        grid_spec=pltpu.PrefetchScalarGridSpec(
            num_scalar_prefetch=1,
            grid=grid,
            in_specs=feat_specs
            + [pl.BlockSpec((group, rows, width), lambda t, _: (0, 0, 0))] * shares,
            out_specs=out_specs,
            scratch_shapes=[pltpu.VMEM((group, width, width), jnp.bfloat16)] * 2 + [swap],
        ),
        **params,
    )(position, features, *parts)


def middle_kernel(owners, group, sources, backs, tile, chained, *refs):
    r_refs = refs[: len(sources)]
    w_ref, feat_ref, cot_ref = refs[len(sources) : len(sources) + 3]
    outs = refs[len(sources) + 3 + chained :]
    layer_ref, part_ref, back_refs = outs[0], outs[1], outs[2:]
    weight = w_ref[0]
    tokens = feat_ref.shape[0]
    depth = weight.shape[0]
    part = None
    for begin in range(0, tokens, tile):
        span = slice(begin, begin + tile)
        first = jnp.concatenate(
            [
                ref[:, unit, 0, :, span].astype(jnp.float32)
                for ref, units in zip(r_refs, sources)
                for unit in range(units)
            ],
            axis=1,
        )
        first = first.reshape(depth, tile).astype(jnp.bfloat16)
        value = contract(first, weight, 0, 0)
        square = value * value
        tangent = jnp.tanh(GELU_SCALE * (value + 0.044715 * square * value))
        half = 0.5 * (1.0 + tangent)
        layer_ref[span, :] = (feat_ref[span, :].astype(jnp.float32) + value * half).astype(
            jnp.bfloat16
        )
        rate = half + 0.5 * value * (1.0 - tangent * tangent) * GELU_SCALE * (
            1.0 + 3.0 * 0.044715 * square
        )
        slope = (cot_ref[span, :].astype(jnp.float32) * rate).astype(jnp.bfloat16)
        back = contract(weight, slope, 1, 1).reshape(owners, depth // owners, tile)
        start = 0
        for units, back_ref in zip(backs, back_refs):
            for unit in range(units):
                back_ref[:, unit, 0, :, span] = back[:, start : start + group].astype(jnp.bfloat16)
                start += group
        term = contract(first, slope, 1, 0)
        part = term if part is None else part + term
    part_ref[0] = part.astype(jnp.bfloat16)


def middle_part(received, w_two, features, cotangent, layer, low, high, backs):
    tokens, columns = features.shape
    owners, _, _, group, _ = received[0][0].shape
    count = high - low
    depth, width = w_two.shape[1:]
    tile = min(256, tokens)
    chained = 0 if layer is None else 1
    column = pl.BlockSpec((tokens, width), lambda j: (0, low + j))
    sources = [array.shape[1] for array, _ in received]
    operands = [array for array, _ in received] + [w_two, features, cotangent]
    operands += [layer] if chained else []

    def spec(units, skipped):
        return pl.BlockSpec(
            (owners, units, 1, group, tokens), lambda j: (0, 0, low - skipped + j, 0, 0)
        )

    return pl.pallas_call(
        functools.partial(middle_kernel, owners, group, sources, backs, tile, chained),
        grid=(count,),
        in_specs=[spec(array.shape[1], skipped) for array, skipped in received]
        + [pl.BlockSpec((1, depth, width), lambda j: (low + j, 0, 0)), column, column]
        + [pl.BlockSpec(memory_space=pl.ANY)] * chained,
        out_specs=[column, pl.BlockSpec((1, depth, width), lambda j: (j, 0, 0))]
        + [spec(units, low) for units in backs],
        out_shape=[
            jax.ShapeDtypeStruct((tokens, columns), jnp.bfloat16),
            jax.ShapeDtypeStruct((count, depth, width), jnp.bfloat16),
        ]
        + [
            jax.ShapeDtypeStruct((owners, units, count, group, tokens), jnp.bfloat16)
            for units in backs
        ],
        input_output_aliases={len(operands) - 1: 0} if chained else {},
        compiler_params=pltpu.CompilerParams(vmem_limit_bytes=VMEM_LIMIT),
        cost_estimate=pl.CostEstimate(
            flops=6 * count * tokens * depth * width,
            bytes_accessed=count * (10 * tokens * width + 4 * depth * width),
            transcendentals=count * tokens * width,
        ),
        name="middle",
    )(*operands)


def last_kernel(held, sources, shares, rows_out, grad_out, chained, position_ref, *refs):
    q_refs, refs = refs[: len(sources)], list(refs[len(sources) :])
    feat_ref = refs.pop(0) if rows_out else None
    w_ref, cot_ref = (refs.pop(0), refs.pop(0)) if grad_out else (None, None)
    refs = refs[chained:]
    keep_ref, send_ref = (refs.pop(0), refs.pop(0)) if rows_out else (None, None)
    grad_ref = refs.pop(0) if grad_out else None
    swap = refs.pop(0)
    total = refs.pop(0) if rows_out else None
    group, tokens = q_refs[0].shape[3:]
    width = swap.shape[1] // (group + 1)
    lanes = tokens // LANES
    step = pl.program_id(0)

    if rows_out:

        @pl.when(step == 0)
        def _():
            total[...] = jnp.zeros_like(total)

    for q_ref, (low, high) in zip(q_refs, sources):
        for owner in range(q_ref.shape[0]):
            for j in range(low, high):
                start = (owner * held + j) * (group + 1)
                for lane in range(lanes):
                    block = q_ref[owner, 0, j - low, :, lane * LANES : (lane + 1) * LANES]
                    swap[lane, pl.ds(start, group), :] = block.astype(jnp.float32)
    for b in range(group):
        back = jnp.concatenate(
            [swap[lane, pl.ds(b, width, stride=group + 1), :] for lane in range(lanes)], axis=1
        ).astype(jnp.bfloat16)
        columns = slice(b * width, (b + 1) * width)
        if grad_out:
            through = contract(back, w_ref[b], 0, 1)
            grad_ref[:, columns] = (cot_ref[:, columns].astype(jnp.float32) + through).astype(
                jnp.bfloat16
            )
        if rows_out:
            total[b] += contract(back, feat_ref[:, columns], 1, 0)

    if rows_out:

        @pl.when(step == pl.num_programs(0) - 1)
        def _():
            rows = width // shares
            me = position_ref[0]
            for b in range(group):
                part = total[b].T.astype(jnp.bfloat16)
                for share in range(shares):
                    mine = (me & 1) == (share & 1)
                    place = (me >> 1) ^ (share >> 1)
                    block = part[share * rows : (share + 1) * rows]

                    @pl.when(mine)
                    def _():
                        keep_ref[place, b] = block

                    @pl.when(jnp.logical_not(mine))
                    def _():
                        send_ref[place, b] = block


def last_part(position, returned, unit, rows_of, grad_of, grad, shares):
    tokens = returned[0][0].shape[-1]
    owners, _, _, group, _ = returned[0][0].shape
    held = sum(array.shape[2] for array, _ in returned)
    width = owners * held
    tile = min(256, tokens)
    strip = pl.BlockSpec((tile, group * width), lambda t, _: (t, unit))
    operands, specs, sources, low = [], [], [], 0
    for array, at in returned:
        count = array.shape[2]
        index_map = functools.partial(lambda at, t, _: (0, at, 0, 0, t), at)
        operands.append(array)
        specs.append(pl.BlockSpec((owners, 1, count, group, tile), index_map))
        sources.append((low, low + count))
        low += count
    outs, out_specs, aliases = [], [], {}
    scratch = [pltpu.VMEM((tile // LANES, width * (group + 1), LANES), jnp.float32)]
    chained = 1 if grad_of is not None and grad is not None else 0
    if rows_of is not None:
        operands.append(rows_of)
        specs.append(strip)
        block = (shares // 2, group, width // shares, width)
        outs += [jax.ShapeDtypeStruct(block, jnp.bfloat16)] * 2
        out_specs += [pl.BlockSpec(block, lambda t, _: (0, 0, 0, 0))] * 2
        scratch.append(pltpu.VMEM((group, width, width), jnp.float32))
    if grad_of is not None:
        w_one, cotangent = grad_of
        operands += [w_one, cotangent]
        specs += [pl.BlockSpec((group, width, width), lambda t, _: (unit, 0, 0)), strip]
        if chained:
            operands.append(grad)
            specs.append(pl.BlockSpec(memory_space=pl.ANY))
            aliases = {len(operands): len(outs)}
        outs.append(jax.ShapeDtypeStruct(cotangent.shape, jnp.bfloat16))
        out_specs.append(strip)
    jobs = (rows_of is not None) + (grad_of is not None)
    return pl.pallas_call(
        functools.partial(
            last_kernel, held, sources, shares, rows_of is not None, grad_of is not None, chained
        ),
        grid_spec=pltpu.PrefetchScalarGridSpec(
            num_scalar_prefetch=1,
            grid=(tokens // tile,),
            in_specs=specs,
            out_specs=out_specs,
            scratch_shapes=scratch,
        ),
        out_shape=outs,
        input_output_aliases=aliases,
        compiler_params=pltpu.CompilerParams(vmem_limit_bytes=VMEM_LIMIT),
        cost_estimate=pl.CostEstimate(
            flops=2 * jobs * group * tokens * width * width,
            bytes_accessed=group * (2 + 3 * jobs) * tokens * width,
            transcendentals=0,
        ),
        name="last",
    )(position, *operands)


def exchange(array, before=None):
    if before is not None:
        array = after(array, before)
    return lax.all_to_all(array, "mp", split_axis=0, concat_axis=0, tiled=True)


def after(array, before):
    return lax.optimization_barrier((array, before))[0]


def swap_with(array, step):
    size = lax.axis_size("dp")
    return lax.ppermute(array, "dp", [(d, d ^ step) for d in range(size)])


def gathered_parts(part):
    parts = [part]
    step = lax.axis_size("dp") // 2
    while step:
        came = [swap_with(array, step) for array in parts]
        parts = [array for pair in zip(parts, came) for array in pair]
        step //= 2
    return parts


def first_hop(keep, send):
    return keep.astype(jnp.float32) + swap_with(send, 1).astype(jnp.float32)


def other_hops(totals):
    total = jnp.concatenate(totals, axis=1)
    count = total.shape[0]
    while count > 1:
        count //= 2
        came = swap_with(total[count:].astype(jnp.bfloat16), 2 * count)
        total = total[:count] + came.astype(jnp.float32)
    return total[0]


def scatter(part):
    return lax.psum_scatter(part, "dp", scatter_dimension=1, tiled=True)


def on_device(features, cotangent, factor_one, factor_two):
    owners = lax.axis_size("mp")
    shares = lax.axis_size("dp")
    held = factor_one.shape[0]
    half = held // 2
    unit = 8 if held % 16 == 0 else held
    units = held // unit

    position = jnp.full((1,), lax.axis_index("dp"), jnp.int32)
    parts = gathered_parts(factor_one[:unit])
    (head,) = first_head(position, features, parts, [(0, held)], owners, held)
    w_one = lax.all_gather(after(factor_one, head), "dp", axis=1, tiled=True)
    w_two = lax.all_gather(after(factor_two, w_one), "dp", axis=1, tiled=True)
    latest = arrived = exchange(head)
    received = [[(arrived, 0)], [(arrived, 0)]]
    if units > 1:
        cuts = [(0, half), (half, held)]
        rest = first_parts(
            after(features, head), w_one, unit, cuts, owners, held, 1, units - 1
        )
        for index, array in enumerate(rest):
            latest = exchange(array, latest)
            received[index].append((latest, index * half))

    backs = [units - 1, 1] if units > 1 else [1]
    layer, part_low, back_low = middle_part(
        received[0], w_two, features, cotangent, None, 0, half, [units]
    )
    latest = back_low = exchange(back_low, latest)
    layer, part_high, *back_high = middle_part(
        received[1], w_two, features, cotangent, layer, half, held, backs
    )
    grad_two = jnp.concatenate([scatter(part_low), scatter(part_high)], axis=0).astype(
        jnp.float32
    )
    for index, array in enumerate(back_high):
        before = (latest, grad_two) if index else latest
        latest = back_high[index] = exchange(array, before)

    grad, hops, parts_one = None, [], []
    for index in range(units):
        final = units > 1 and index == units - 1
        back, at = (back_high[1], 0) if final else (back_high[0], index)
        if final:
            back = after(back, parts_one)
        returned = [(back_low, index), (back, at)]
        grad_of = (w_one, cotangent)
        if final:
            keep, send = last_part(position, returned, index, features, None, None, shares)
            (grad,) = last_part(position, returned, index, None, grad_of, grad, shares)
        else:
            keep, send, grad = last_part(
                position, returned, index, features, grad_of, grad, shares
            )
        hops.append(first_hop(keep, send))
        if index == units - 3:
            parts_one.append(other_hops(hops))
        elif index >= units - 2:
            parts_one.append(other_hops(hops[-1:]))
    grad_one = jnp.concatenate(parts_one[:-1] + [jnp.zeros_like(parts_one[-1])], axis=0)
    start = held - parts_one[-1].shape[0]
    grad_one = lax.dynamic_update_slice(grad_one, parts_one[-1], (start, 0, 0))
    return (
        layer,
        grad,
        grad_one,
        grad_two,
    )


def solution(mesh):
    in_specs = (P("dp", "mp"), P("dp", "mp"), P("mp", "dp", None), P("mp", "dp", None))
    out_specs = (P("dp", "mp"), P("dp", "mp"), P("mp", "dp", None), P("mp", "dp", None))
    return jax.shard_map(
        on_device, mesh=mesh, in_specs=in_specs, out_specs=out_specs, check_vma=False
    )
```

```python
import functools
import math

import jax
import jax.numpy as jnp
from jax import lax
from jax.experimental import pallas as pl
from jax.experimental.pallas import tpu as pltpu
from jax.sharding import PartitionSpec as P

LANES = 128
VMEM_LIMIT = 60 * 1024 * 1024
MIDDLE_COST = 6
GELU_SCALE = math.sqrt(2.0 / math.pi)


def contract(left, right, left_axis, right_axis):
    return lax.dot_general(
        left, right, (((left_axis,), (right_axis,)), ((), ())), preferred_element_type=jnp.float32
    )


def bundled(arrays, sizes):
    arrays, bundles = list(arrays), []
    for size in sizes:
        bundles.append(arrays[:size])
        arrays = arrays[size:]
    return bundles


def owners_of(place_ref, step, size, owners):
    return range(owners) if size == 1 else [place_ref[1] ^ step]


def rows_at(start, size):
    return pl.ds(start if isinstance(start, int) else pl.multiple_of(start, 8), size)


def first_rows(place_ref, feat_ref, weight, out_refs, unit, cuts, owners, held, swap):
    tokens = feat_ref.shape[0]
    group, width, _ = weight.shape
    for b in range(group):
        rows = contract(weight[b], feat_ref[:, b * width : (b + 1) * width], 1, 1)
        for lane in range(tokens // LANES):
            swap[lane, pl.ds(b, width, stride=group), :] = rows[
                :, lane * LANES : (lane + 1) * LANES
            ]
    spots = [(low, high, step, size) for low, high, size in cuts for step in range(size)]
    for out_ref, (low, high, step, size) in zip(out_refs, spots):
        for index, owner in enumerate(owners_of(place_ref, step, size, owners)):
            start = (owner * held + low) * group
            for lane in range(tokens // LANES):
                block = swap[lane, rows_at(start, (high - low) * group), :]
                out_ref[index, unit, :, :, lane * LANES : (lane + 1) * LANES] = block.reshape(
                    high - low, group, LANES
                ).astype(jnp.bfloat16)


def first_kernel(cuts, owners, held, units, place_ref, *refs):
    feat_refs, w_refs, out_refs = refs[:units], refs[units : 2 * units], refs[2 * units : -2]
    weight, swap = refs[-2:]

    @pl.when(pl.program_id(0) == 0)
    def _():
        for unit, w_ref in enumerate(w_refs):
            for b in range(w_ref.shape[0]):
                weight[unit, b] = w_ref[b].T

    for unit in range(units):
        first_rows(
            place_ref,
            feat_refs[unit],
            weight.at[unit],
            out_refs,
            unit,
            cuts,
            owners,
            held,
            swap,
        )


def head_kernel(cuts, owners, held, shares, place_ref, feat_ref, *refs):
    part_refs, gathered, weight, swap = refs[:shares], *refs[-3:]
    rows = weight.shape[1] // shares

    @pl.when(pl.program_id(0) == 0)
    def _():
        for step, part_ref in enumerate(part_refs):
            start = pl.multiple_of((place_ref[0] ^ step) * rows, rows)
            gathered[:, pl.ds(start, rows), :] = part_ref[...]
        for b in range(weight.shape[0]):
            weight[b] = gathered[b].T

    first_rows(place_ref, feat_ref, weight, refs[shares:-3], 0, cuts, owners, held, swap)


def first_call(features, group, width, cuts, owners, begin, units):
    tokens = features.shape[0]
    tile = min(256, tokens)
    outs = [
        jax.ShapeDtypeStruct((owners // size, units, high - low, group, tokens), jnp.bfloat16)
        for low, high, size in cuts
        for _ in range(size)
    ]
    moved = 2 * units * (tokens * group * width + group * width * width)
    moved += sum(2 * math.prod(out.shape) for out in outs)
    feat_specs = [
        pl.BlockSpec((tile, group * width), functools.partial(lambda u, t, *_: (t, u), begin + u))
        for u in range(units)
    ]
    out_specs = [
        pl.BlockSpec(
            (owners // size, units, high - low, group, tile), lambda t, *_: (0, 0, 0, 0, t)
        )
        for low, high, size in cuts
        for _ in range(size)
    ]
    swap = pltpu.VMEM((tile // LANES, width * group, LANES), jnp.float32)
    params = dict(
        out_shape=outs,
        compiler_params=pltpu.CompilerParams(vmem_limit_bytes=VMEM_LIMIT),
        cost_estimate=pl.CostEstimate(
            flops=2 * units * tokens * group * width * width,
            bytes_accessed=moved,
            transcendentals=0,
        ),
        name="first",
    )
    return (tokens // tile,), feat_specs, out_specs, swap, params


def first_parts(places, features, w_one, group, cuts, owners, held, begin, units):
    width = w_one.shape[1]
    grid, feat_specs, out_specs, swap, params = first_call(
        features, group, width, cuts, owners, begin, units
    )
    w_specs = [
        pl.BlockSpec((group, width, width), functools.partial(lambda u, t, _: (u, 0, 0), begin + u))
        for u in range(units)
    ]
    results = pl.pallas_call(
        functools.partial(first_kernel, cuts, owners, held, units),
        grid_spec=pltpu.PrefetchScalarGridSpec(
            num_scalar_prefetch=1,
            grid=grid,
            in_specs=feat_specs + w_specs,
            out_specs=out_specs,
            scratch_shapes=[pltpu.VMEM((units, group, width, width), jnp.bfloat16), swap],
        ),
        **params,
    )(places, *[features] * units, *[w_one] * units)
    return bundled(results, [size for _, _, size in cuts])


def first_head(places, features, parts, cuts, owners, held):
    group, rows, width = parts[0].shape
    shares = len(parts)
    grid, feat_specs, out_specs, swap, params = first_call(
        features, group, width, cuts, owners, 0, 1
    )
    return pl.pallas_call(
        functools.partial(head_kernel, cuts, owners, held, shares),
        grid_spec=pltpu.PrefetchScalarGridSpec(
            num_scalar_prefetch=1,
            grid=grid,
            in_specs=feat_specs
            + [pl.BlockSpec((group, rows, width), lambda t, _: (0, 0, 0))] * shares,
            out_specs=out_specs,
            scratch_shapes=[pltpu.VMEM((group, width, width), jnp.bfloat16)] * 2 + [swap],
        ),
        **params,
    )(places, features, *parts)


def middle_kernel(owners, group, parts, sources, backs, tile, chained, place_ref, *refs):
    count = sum(size for _, size in sources)
    r_bundles = bundled(refs[:count], [size for _, size in sources])
    w_ref, feat_ref, cot_ref = refs[count : count + 3]
    layer_ref, part_ref, *outs = refs[count + 3 + chained :]
    back_bundles = bundled(outs, [size for _, size in backs])
    tokens = feat_ref.shape[0]
    depth = w_ref.shape[1]
    held = depth // owners

    def pick(bundle, step):
        if len(bundle) > 1 or parts == 1:
            return bundle[step], slice(None)
        return bundle[0], pl.ds(place_ref[1] ^ step, 1)

    if parts == 1:
        spots = [slice(None)]
    else:
        spots = [
            pl.ds(pl.multiple_of((place_ref[1] ^ step) * held, held), held) for step in range(parts)
        ]
    weight = jnp.concatenate([w_ref[0, spot, :] for spot in spots], axis=0)
    part = None
    for begin in range(0, tokens, tile):
        span = slice(begin, begin + tile)
        pieces = []
        for step in range(parts):
            blocks = []
            for (units, _), bundle in zip(sources, r_bundles):
                ref, at = pick(bundle, step)
                blocks += [ref[at, u, 0, :, span].astype(jnp.float32) for u in range(units)]
            pieces.append(jnp.concatenate(blocks, axis=1))
        first = jnp.concatenate(pieces, axis=0).reshape(depth, tile).astype(jnp.bfloat16)
        value = contract(first, weight, 0, 0)
        square = value * value
        tangent = jnp.tanh(GELU_SCALE * (value + 0.044715 * square * value))
        half = 0.5 * (1.0 + tangent)
        layer_ref[span, :] = (feat_ref[span, :].astype(jnp.float32) + value * half).astype(
            jnp.bfloat16
        )
        rate = half + 0.5 * value * (1.0 - tangent * tangent) * GELU_SCALE * (
            1.0 + 3.0 * 0.044715 * square
        )
        slope = (cot_ref[span, :].astype(jnp.float32) * rate).astype(jnp.bfloat16)
        back = contract(weight, slope, 1, 1).reshape(parts, owners // parts, held, tile)
        for step in range(parts):
            start = 0
            for (units, _), bundle in zip(backs, back_bundles):
                ref, at = pick(bundle, step)
                for u in range(units):
                    ref[at, u, 0, :, span] = back[step, :, start : start + group].astype(
                        jnp.bfloat16
                    )
                    start += group
        term = contract(first, slope, 1, 0)
        part = term if part is None else part + term
    part = part.astype(jnp.bfloat16)
    rows = depth // parts
    for step, spot in enumerate(spots):
        part_ref[0, spot, :] = part[step * rows : (step + 1) * rows]


def middle_part(places, received, w_two, features, cotangent, layer, low, high, backs, parts):
    tokens, columns = features.shape
    group = received[0][0][0].shape[3]
    owners = sum(array.shape[0] for array in received[0][0])
    count = high - low
    depth, width = w_two.shape[1:]
    tile = min(256, tokens)
    chained = 0 if layer is None else 1
    column = pl.BlockSpec((tokens, width), lambda j, _: (0, low + j))
    sources = [(bundle[0].shape[1], len(bundle)) for bundle, _ in received]
    operands = [array for bundle, _ in received for array in bundle]
    operands += [w_two, features, cotangent] + ([layer] if chained else [])

    def specs(units, size, skipped):
        block = (owners // size, units, 1, group, tokens)
        return [pl.BlockSpec(block, lambda j, _: (0, 0, low - skipped + j, 0, 0))] * size

    results = pl.pallas_call(
        functools.partial(middle_kernel, owners, group, parts, sources, backs, tile, chained),
        grid_spec=pltpu.PrefetchScalarGridSpec(
            num_scalar_prefetch=1,
            grid=(count,),
            in_specs=[
                spec
                for (units, size), (_, skipped) in zip(sources, received)
                for spec in specs(units, size, skipped)
            ]
            + [pl.BlockSpec((1, depth, width), lambda j, _: (low + j, 0, 0)), column, column]
            + [pl.BlockSpec(memory_space=pl.ANY)] * chained,
            out_specs=[column, pl.BlockSpec((1, depth, width), lambda j, _: (j, 0, 0))]
            + [spec for units, size in backs for spec in specs(units, size, low)],
        ),
        out_shape=[
            jax.ShapeDtypeStruct((tokens, columns), jnp.bfloat16),
            jax.ShapeDtypeStruct((count, depth, width), jnp.bfloat16),
        ]
        + [
            jax.ShapeDtypeStruct((owners // size, units, count, group, tokens), jnp.bfloat16)
            for units, size in backs
            for _ in range(size)
        ],
        input_output_aliases={len(operands): 0} if chained else {},
        compiler_params=pltpu.CompilerParams(vmem_limit_bytes=VMEM_LIMIT),
        cost_estimate=pl.CostEstimate(
            flops=MIDDLE_COST * count * tokens * depth * width,
            bytes_accessed=count * (10 * tokens * width + 4 * depth * width),
            transcendentals=count * tokens * width,
        ),
        name="middle",
    )(places, *operands)
    return results[0], results[1], *bundled(results[2:], [size for _, size in backs])


def last_kernel(owners, held, sources, shares, rows_out, grad_out, chained, place_ref, *refs):
    q_refs, refs = refs[: len(sources)], list(refs[len(sources) :])
    feat_ref = refs.pop(0) if rows_out else None
    w_ref, cot_ref = (refs.pop(0), refs.pop(0)) if grad_out else (None, None)
    refs = refs[chained:]
    keep_ref, send_ref = (refs.pop(0), refs.pop(0)) if rows_out else (None, None)
    grad_ref = refs.pop(0) if grad_out else None
    swap = refs.pop(0)
    total = refs.pop(0) if rows_out else None
    group, tokens = q_refs[0].shape[3:]
    width = swap.shape[1] // group
    lanes = tokens // LANES
    step = pl.program_id(0)

    if rows_out:

        @pl.when(step == 0)
        def _():
            total[...] = jnp.zeros_like(total)

    for q_ref, (low, high, chunk, size) in zip(q_refs, sources):
        for index, owner in enumerate(owners_of(place_ref, chunk, size, owners)):
            start = (owner * held + low) * group
            for lane in range(lanes):
                block = q_ref[index, 0, :, :, lane * LANES : (lane + 1) * LANES]
                swap[lane, rows_at(start, (high - low) * group), :] = block.astype(
                    jnp.float32
                ).reshape((high - low) * group, LANES)
    for b in range(group):
        back = jnp.concatenate(
            [swap[lane, pl.ds(b, width, stride=group), :] for lane in range(lanes)], axis=1
        ).astype(jnp.bfloat16)
        columns = slice(b * width, (b + 1) * width)
        if grad_out:
            through = contract(back, w_ref[b], 0, 1)
            grad_ref[:, columns] = (cot_ref[:, columns].astype(jnp.float32) + through).astype(
                jnp.bfloat16
            )
        if rows_out:
            total[b] += contract(back, feat_ref[:, columns], 1, 0)

    if rows_out:

        @pl.when(step == pl.num_programs(0) - 1)
        def _():
            rows = width // shares
            me = place_ref[0]
            for b in range(group):
                part = total[b].T.astype(jnp.bfloat16)
                for share in range(shares):
                    mine = (me & 1) == (share & 1)
                    place = (me >> 1) ^ (share >> 1)
                    block = part[share * rows : (share + 1) * rows]

                    @pl.when(mine)
                    def _():
                        keep_ref[place, b] = block

                    @pl.when(jnp.logical_not(mine))
                    def _():
                        send_ref[place, b] = block


def last_part(places, returned, unit, rows_of, grad_of, grad, shares):
    group, tokens = returned[0][0][0].shape[3:]
    owners = sum(array.shape[0] for array in returned[0][0])
    held = sum(bundle[0].shape[2] for bundle, _ in returned)
    width = owners * held
    tile = min(256, tokens)
    strip = pl.BlockSpec((tile, group * width), lambda t, _: (t, unit))
    operands, specs, sources, low = [], [], [], 0
    for bundle, at in returned:
        count = bundle[0].shape[2]
        index_map = functools.partial(lambda at, t, _: (0, at, 0, 0, t), at)
        for chunk, array in enumerate(bundle):
            operands.append(array)
            specs.append(pl.BlockSpec((array.shape[0], 1, count, group, tile), index_map))
            sources.append((low, low + count, chunk, len(bundle)))
        low += count
    outs, out_specs, aliases = [], [], {}
    scratch = [pltpu.VMEM((tile // LANES, width * group, LANES), jnp.float32)]
    chained = 1 if grad_of is not None and grad is not None else 0
    if rows_of is not None:
        operands.append(rows_of)
        specs.append(strip)
        block = (shares // 2, group, width // shares, width)
        outs += [jax.ShapeDtypeStruct(block, jnp.bfloat16)] * 2
        out_specs += [pl.BlockSpec(block, lambda t, _: (0, 0, 0, 0))] * 2
        scratch.append(pltpu.VMEM((group, width, width), jnp.float32))
    if grad_of is not None:
        w_one, cotangent = grad_of
        operands += [w_one, cotangent]
        specs += [pl.BlockSpec((group, width, width), lambda t, _: (unit, 0, 0)), strip]
        if chained:
            operands.append(grad)
            specs.append(pl.BlockSpec(memory_space=pl.ANY))
            aliases = {len(operands): len(outs)}
        outs.append(jax.ShapeDtypeStruct(cotangent.shape, jnp.bfloat16))
        out_specs.append(strip)
    jobs = (rows_of is not None) + (grad_of is not None)
    return pl.pallas_call(
        functools.partial(
            last_kernel,
            owners,
            held,
            sources,
            shares,
            rows_of is not None,
            grad_of is not None,
            chained,
        ),
        grid_spec=pltpu.PrefetchScalarGridSpec(
            num_scalar_prefetch=1,
            grid=(tokens // tile,),
            in_specs=specs,
            out_specs=out_specs,
            scratch_shapes=scratch,
        ),
        out_shape=outs,
        input_output_aliases=aliases,
        compiler_params=pltpu.CompilerParams(vmem_limit_bytes=VMEM_LIMIT),
        cost_estimate=pl.CostEstimate(
            flops=2 * jobs * group * tokens * width * width,
            bytes_accessed=group * (2 + 3 * jobs) * tokens * width,
            transcendentals=0,
        ),
        name="last",
    )(places, *operands)


def exchange(array, before=None):
    if before is not None:
        array = after(array, before)
    return lax.all_to_all(array, "mp", split_axis=0, concat_axis=0, tiled=True)


def after(array, before):
    return lax.optimization_barrier((array, before))[0]


def exchange_by_partner(bundle):
    size = len(bundle)
    came = list(bundle)
    for step in range(1, size):
        came[step] = lax.ppermute(bundle[step], "mp", [(d, d ^ step) for d in range(size)])
    return came


def swap_with(array, step):
    size = lax.axis_size("dp")
    return lax.ppermute(array, "dp", [(d, d ^ step) for d in range(size)])


def gathered_parts(part):
    parts = [part]
    step = lax.axis_size("dp") // 2
    while step:
        came = [swap_with(array, step) for array in parts]
        parts = [array for pair in zip(parts, came) for array in pair]
        step //= 2
    return parts


def first_hop(keep, send):
    return keep.astype(jnp.float32) + swap_with(send, 1).astype(jnp.float32)


def other_hops(totals):
    total = jnp.concatenate(totals, axis=1)
    count = total.shape[0]
    while count > 1:
        count //= 2
        came = swap_with(total[count:].astype(jnp.bfloat16), 2 * count)
        total = total[:count] + came.astype(jnp.float32)
    return total[0]


def scatter(part):
    return lax.psum_scatter(part, "dp", scatter_dimension=1, tiled=True)


def on_device(features, cotangent, factor_one, factor_two):
    owners = lax.axis_size("mp")
    shares = lax.axis_size("dp")
    held = factor_one.shape[0]
    half = held // 2
    unit = 8 if held % 16 == 0 else held
    units = held // unit

    places = jnp.stack([lax.axis_index("dp"), lax.axis_index("mp")]).astype(jnp.int32)
    shards = gathered_parts(factor_one[:unit])
    (head,) = first_head(places, features, shards, [(0, held, 1)], owners, held)
    w_one = lax.all_gather(after(factor_one, head), "dp", axis=1, tiled=True)
    w_two = lax.all_gather(after(factor_two, w_one), "dp", axis=1, tiled=True)
    latest = arrived = exchange(head)
    received = [[([arrived], 0)], [([arrived], 0)]]
    parts = owners if units > 1 and owners & (owners - 1) == 0 else 1
    if units > 1:
        cuts = [(0, half, parts), (half, held, 1)]
        low_rows, (high_rows,) = first_parts(
            places, after(features, head), w_one, unit, cuts, owners, held, 1, units - 1
        )
        if parts > 1:
            low_rows = exchange_by_partner(low_rows)
            received[0].append((low_rows, 0))
            latest = (latest, low_rows[parts // 2], low_rows[parts // 2 + 1])
        else:
            latest = exchange(low_rows[0], latest)
            received[0].append(([latest], 0))
        latest = exchange(high_rows, latest)
        received[1].append(([latest], half))

    backs = [(units - 1, 1), (1, 1)] if units > 1 else [(1, 1)]
    layer, part_low, back_low = middle_part(
        places,
        received[0],
        w_two,
        features,
        cotangent,
        None,
        0,
        half,
        [(units, parts)],
        parts,
    )
    if parts > 1:
        back_low = exchange_by_partner(back_low)
        latest = (latest, back_low)
    else:
        latest = exchange(back_low[0], latest)
        back_low = [latest]
    layer, part_high, *back_high = middle_part(
        places, received[1], w_two, features, cotangent, layer, half, held, backs, parts
    )
    parts_two = [scatter(part_low), scatter(part_high)]
    for index, (array,) in enumerate(back_high):
        before = (latest, parts_two) if index else latest
        latest = back_high[index] = exchange(array, before)

    grad, hops, parts_one = None, [], []
    for index in range(units):
        final = units > 1 and index == units - 1
        back, at = (back_high[1], 0) if final else (back_high[0], index)
        if final:
            back = after(back, parts_one)
        returned = [(back_low, index), ([back], at)]
        grad_of = (w_one, cotangent)
        if final:
            keep, send = last_part(places, returned, index, features, None, None, shares)
            (grad,) = last_part(places, returned, index, None, grad_of, grad, shares)
        else:
            keep, send, grad = last_part(places, returned, index, features, grad_of, grad, shares)
        hops.append(first_hop(keep, send))
        if index == units // 2 - 1 or index == units - 1:
            parts_one.append(other_hops(hops[-(units // 2 or 1) :]))
    parts_two = after(parts_two, hops[-1])
    grad_one = jnp.concatenate(parts_one[:-1] + [jnp.zeros_like(parts_one[-1])], axis=0)
    start = held - parts_one[-1].shape[0]
    grad_one = lax.dynamic_update_slice(grad_one, parts_one[-1], (start, 0, 0))
    return (
        layer,
        grad,
        grad_one,
        jnp.concatenate(parts_two, axis=0).astype(jnp.float32),
    )


def solution(mesh):
    in_specs = (P("dp", "mp"), P("dp", "mp"), P("mp", "dp", None), P("mp", "dp", None))
    out_specs = (P("dp", "mp"), P("dp", "mp"), P("mp", "dp", None), P("mp", "dp", None))
    return jax.shard_map(
        on_device, mesh=mesh, in_specs=in_specs, out_specs=out_specs, check_vma=False
    )
```

```python
import functools
import math

import jax
import jax.numpy as jnp
from jax import lax
from jax.experimental import pallas as pl
from jax.experimental.pallas import tpu as pltpu
from jax.sharding import PartitionSpec as P

LANES = 128
VMEM_LIMIT = 125 * 512 * 1024
GELU_SCALE = math.sqrt(2.0 / math.pi)


def contract(left, right, left_axis, right_axis):
    return lax.dot_general(
        left, right, (((left_axis,), (right_axis,)), ((), ())), preferred_element_type=jnp.float32
    )


def first_rows(feat_ref, weight, out_refs, unit, cuts, owners, held, swap):
    tokens = feat_ref.shape[0]
    group, width, _ = weight.shape
    for b in range(group):
        rows = contract(weight[b], feat_ref[:, b * width : (b + 1) * width], 1, 1)
        for lane in range(tokens // LANES):
            swap[lane, pl.ds(b, width, stride=group), :] = rows[
                :, lane * LANES : (lane + 1) * LANES
            ]
    for out_ref, (low, high) in zip(out_refs, cuts):
        for owner in range(owners):
            start = (owner * held + low) * group
            for lane in range(tokens // LANES):
                block = swap[lane, pl.ds(start, (high - low) * group), :]
                out_ref[owner, unit, :, :, lane * LANES : (lane + 1) * LANES] = block.reshape(
                    high - low, group, LANES
                ).astype(jnp.bfloat16)


def first_kernel(cuts, owners, held, units, *refs):
    feat_refs, w_refs, out_refs = refs[:units], refs[units : 2 * units], refs[2 * units : -2]
    weight, swap = refs[-2:]

    @pl.when(pl.program_id(0) == 0)
    def _():
        for unit, w_ref in enumerate(w_refs):
            for b in range(w_ref.shape[0]):
                weight[unit, b] = w_ref[b].T

    for unit in range(units):
        first_rows(feat_refs[unit], weight.at[unit], out_refs, unit, cuts, owners, held, swap)


def head_kernel(cuts, owners, held, shares, position_ref, feat_ref, *refs):
    part_refs, gathered, weight, swap = refs[:shares], *refs[-3:]
    rows = weight.shape[1] // shares

    @pl.when(pl.program_id(0) == 0)
    def _():
        for step, part_ref in enumerate(part_refs):
            start = pl.multiple_of((position_ref[0] ^ step) * rows, rows)
            gathered[:, pl.ds(start, rows), :] = part_ref[...]
        for b in range(weight.shape[0]):
            weight[b] = gathered[b].T

    first_rows(feat_ref, weight, refs[shares:-3], 0, cuts, owners, held, swap)


def first_call(features, group, width, cuts, owners, begin, units):
    tokens = features.shape[0]
    tile = min(256, tokens)
    outs = [
        jax.ShapeDtypeStruct((owners, units, high - low, group, tokens), jnp.bfloat16)
        for low, high in cuts
    ]
    moved = 2 * units * (tokens * group * width + group * width * width)
    moved += sum(2 * math.prod(out.shape) for out in outs)
    feat_specs = [
        pl.BlockSpec((tile, group * width), functools.partial(lambda u, t, *_: (t, u), begin + u))
        for u in range(units)
    ]
    out_specs = [
        pl.BlockSpec((owners, units, high - low, group, tile), lambda t, *_: (0, 0, 0, 0, t))
        for low, high in cuts
    ]
    swap = pltpu.VMEM((tile // LANES, width * group, LANES), jnp.float32)
    params = dict(
        out_shape=outs,
        compiler_params=pltpu.CompilerParams(vmem_limit_bytes=VMEM_LIMIT),
        cost_estimate=pl.CostEstimate(
            flops=2 * units * tokens * group * width * width,
            bytes_accessed=moved,
            transcendentals=0,
        ),
        name="first",
    )
    return (tokens // tile,), feat_specs, out_specs, swap, params


def first_parts(features, w_one, group, cuts, owners, held, begin, units):
    width = w_one.shape[1]
    grid, feat_specs, out_specs, swap, params = first_call(
        features, group, width, cuts, owners, begin, units
    )
    w_specs = [
        pl.BlockSpec((group, width, width), functools.partial(lambda u, t: (u, 0, 0), begin + u))
        for u in range(units)
    ]
    return pl.pallas_call(
        functools.partial(first_kernel, cuts, owners, held, units),
        grid=grid,
        in_specs=feat_specs + w_specs,
        out_specs=out_specs,
        scratch_shapes=[pltpu.VMEM((units, group, width, width), jnp.bfloat16), swap],
        **params,
    )(*[features] * units, *[w_one] * units)


def first_head(position, features, parts, cuts, owners, held):
    group, rows, width = parts[0].shape
    shares = len(parts)
    grid, feat_specs, out_specs, swap, params = first_call(
        features, group, width, cuts, owners, 0, 1
    )
    return pl.pallas_call(
        functools.partial(head_kernel, cuts, owners, held, shares),
        grid_spec=pltpu.PrefetchScalarGridSpec(
            num_scalar_prefetch=1,
            grid=grid,
            in_specs=feat_specs
            + [pl.BlockSpec((group, rows, width), lambda t, _: (0, 0, 0))] * shares,
            out_specs=out_specs,
            scratch_shapes=[pltpu.VMEM((group, width, width), jnp.bfloat16)] * 2 + [swap],
        ),
        **params,
    )(position, features, *parts)


def middle_kernel(owners, group, sources, backs, tile, chained, *refs):
    r_refs = refs[: len(sources)]
    w_ref, feat_ref, cot_ref = refs[len(sources) : len(sources) + 3]
    outs = refs[len(sources) + 3 + chained :]
    layer_ref, part_ref, back_refs = outs[0], outs[1], outs[2:]
    weight = w_ref[0]
    tokens = feat_ref.shape[0]
    depth = weight.shape[0]
    part = None
    for begin in range(0, tokens, tile):
        span = slice(begin, begin + tile)
        first = jnp.concatenate(
            [
                ref[:, unit, 0, :, span].astype(jnp.float32)
                for ref, units in zip(r_refs, sources)
                for unit in range(units)
            ],
            axis=1,
        )
        first = first.reshape(depth, tile).astype(jnp.bfloat16)
        value = contract(first, weight, 0, 0)
        square = value * value
        tangent = jnp.tanh(GELU_SCALE * (value + 0.044715 * square * value))
        half = 0.5 * (1.0 + tangent)
        layer_ref[span, :] = (feat_ref[span, :].astype(jnp.float32) + value * half).astype(
            jnp.bfloat16
        )
        rate = half + 0.5 * value * (1.0 - tangent * tangent) * GELU_SCALE * (
            1.0 + 3.0 * 0.044715 * square
        )
        slope = (cot_ref[span, :].astype(jnp.float32) * rate).astype(jnp.bfloat16)
        back = contract(weight, slope, 1, 1).reshape(owners, depth // owners, tile)
        start = 0
        for units, back_ref in zip(backs, back_refs):
            for unit in range(units):
                back_ref[:, unit, 0, :, span] = back[:, start : start + group].astype(jnp.bfloat16)
                start += group
        term = contract(first, slope, 1, 0)
        part = term if part is None else part + term
    part_ref[0] = part.astype(jnp.bfloat16)


def middle_part(received, w_two, features, cotangent, layer, low, high, backs):
    tokens, columns = features.shape
    owners, _, _, group, _ = received[0][0].shape
    count = high - low
    depth, width = w_two.shape[1:]
    tile = min(256, tokens)
    chained = 0 if layer is None else 1
    column = pl.BlockSpec((tokens, width), lambda j: (0, low + j))
    sources = [array.shape[1] for array, _ in received]
    operands = [array for array, _ in received] + [w_two, features, cotangent]
    operands += [layer] if chained else []

    def spec(units, skipped):
        return pl.BlockSpec(
            (owners, units, 1, group, tokens), lambda j: (0, 0, low - skipped + j, 0, 0)
        )

    return pl.pallas_call(
        functools.partial(middle_kernel, owners, group, sources, backs, tile, chained),
        grid=(count,),
        in_specs=[spec(array.shape[1], skipped) for array, skipped in received]
        + [pl.BlockSpec((1, depth, width), lambda j: (low + j, 0, 0)), column, column]
        + [pl.BlockSpec(memory_space=pl.ANY)] * chained,
        out_specs=[column, pl.BlockSpec((1, depth, width), lambda j: (j, 0, 0))]
        + [spec(units, low) for units in backs],
        out_shape=[
            jax.ShapeDtypeStruct((tokens, columns), jnp.bfloat16),
            jax.ShapeDtypeStruct((count, depth, width), jnp.bfloat16),
        ]
        + [
            jax.ShapeDtypeStruct((owners, units, count, group, tokens), jnp.bfloat16)
            for units in backs
        ],
        input_output_aliases={len(operands) - 1: 0} if chained else {},
        compiler_params=pltpu.CompilerParams(vmem_limit_bytes=VMEM_LIMIT),
        cost_estimate=pl.CostEstimate(
            flops=6 * count * tokens * depth * width,
            bytes_accessed=count * (10 * tokens * width + 4 * depth * width),
            transcendentals=count * tokens * width,
        ),
        name="middle",
    )(*operands)


def last_kernel(held, sources, shares, rows_out, grad_out, chained, position_ref, *refs):
    q_refs, refs = refs[: len(sources)], list(refs[len(sources) :])
    feat_ref = refs.pop(0) if rows_out else None
    w_ref, cot_ref = (refs.pop(0), refs.pop(0)) if grad_out else (None, None)
    refs = refs[chained:]
    keep_ref, send_ref = (refs.pop(0), refs.pop(0)) if rows_out else (None, None)
    grad_ref = refs.pop(0) if grad_out else None
    swap = refs.pop(0)
    total = refs.pop(0) if rows_out else None
    group, tokens = q_refs[0].shape[3:]
    width = swap.shape[1] // group
    lanes = tokens // LANES
    step = pl.program_id(0)

    if rows_out:

        @pl.when(step == 0)
        def _():
            total[...] = jnp.zeros_like(total)

    for q_ref, (low, high) in zip(q_refs, sources):
        for owner in range(q_ref.shape[0]):
            start = (owner * held + low) * group
            for lane in range(lanes):
                block = q_ref[owner, 0, :, :, lane * LANES : (lane + 1) * LANES]
                swap[lane, pl.ds(start, (high - low) * group), :] = block.astype(
                    jnp.float32
                ).reshape((high - low) * group, LANES)
    for b in range(group):
        back = jnp.concatenate(
            [swap[lane, pl.ds(b, width, stride=group), :] for lane in range(lanes)], axis=1
        ).astype(jnp.bfloat16)
        columns = slice(b * width, (b + 1) * width)
        if grad_out:
            through = contract(back, w_ref[b], 0, 1)
            grad_ref[:, columns] = (cot_ref[:, columns].astype(jnp.float32) + through).astype(
                jnp.bfloat16
            )
        if rows_out:
            total[b] += contract(back, feat_ref[:, columns], 1, 0)

    if rows_out:

        @pl.when(step == pl.num_programs(0) - 1)
        def _():
            rows = width // shares
            me = position_ref[0]
            for parity in range(2):

                @pl.when((me & 1) == parity)
                def _():
                    for b in range(group):
                        part = total[b].T.astype(jnp.bfloat16)
                        for share in range(shares):
                            ref = keep_ref if share & 1 == parity else send_ref
                            ref[(me >> 1) ^ (share >> 1), b] = part[
                                share * rows : (share + 1) * rows
                            ]


def last_part(position, returned, unit, rows_of, grad_of, grad, shares):
    tokens = returned[0][0].shape[-1]
    owners, _, _, group, _ = returned[0][0].shape
    held = sum(array.shape[2] for array, _ in returned)
    width = owners * held
    tile = min(256, tokens)
    strip = pl.BlockSpec((tile, group * width), lambda t, _: (t, unit))
    operands, specs, sources, low = [], [], [], 0
    for array, at in returned:
        count = array.shape[2]
        index_map = functools.partial(lambda at, t, _: (0, at, 0, 0, t), at)
        operands.append(array)
        specs.append(pl.BlockSpec((owners, 1, count, group, tile), index_map))
        sources.append((low, low + count))
        low += count
    outs, out_specs, aliases = [], [], {}
    scratch = [pltpu.VMEM((tile // LANES, width * group, LANES), jnp.float32)]
    chained = 1 if grad_of is not None and grad is not None else 0
    if rows_of is not None:
        operands.append(rows_of)
        specs.append(strip)
        block = (shares // 2, group, width // shares, width)
        outs += [jax.ShapeDtypeStruct(block, jnp.bfloat16)] * 2
        out_specs += [pl.BlockSpec(block, lambda t, _: (0, 0, 0, 0))] * 2
        scratch.append(pltpu.VMEM((group, width, width), jnp.float32))
    if grad_of is not None:
        w_one, cotangent = grad_of
        operands += [w_one, cotangent]
        specs += [pl.BlockSpec((group, width, width), lambda t, _: (unit, 0, 0)), strip]
        if chained:
            operands.append(grad)
            specs.append(pl.BlockSpec(memory_space=pl.ANY))
            aliases = {len(operands): len(outs)}
        outs.append(jax.ShapeDtypeStruct(cotangent.shape, jnp.bfloat16))
        out_specs.append(strip)
    jobs = (rows_of is not None) + (grad_of is not None)
    return pl.pallas_call(
        functools.partial(
            last_kernel, held, sources, shares, rows_of is not None, grad_of is not None, chained
        ),
        grid_spec=pltpu.PrefetchScalarGridSpec(
            num_scalar_prefetch=1,
            grid=(tokens // tile,),
            in_specs=specs,
            out_specs=out_specs,
            scratch_shapes=scratch,
        ),
        out_shape=outs,
        input_output_aliases=aliases,
        compiler_params=pltpu.CompilerParams(vmem_limit_bytes=VMEM_LIMIT),
        cost_estimate=pl.CostEstimate(
            flops=2 * jobs * group * tokens * width * width,
            bytes_accessed=group * (2 + 3 * jobs) * tokens * width,
            transcendentals=0,
        ),
        name="last",
    )(position, *operands)


def exchange(array, before=None):
    if before is not None:
        array = after(array, before)
    return lax.all_to_all(array, "mp", split_axis=0, concat_axis=0, tiled=True)


def after(array, before):
    return lax.optimization_barrier((array, before))[0]


def swap_with(array, step):
    size = lax.axis_size("dp")
    return lax.ppermute(array, "dp", [(d, d ^ step) for d in range(size)])


def gathered_parts(part):
    parts = [part]
    step = lax.axis_size("dp") // 2
    while step:
        came = [swap_with(array, step) for array in parts]
        parts = [array for pair in zip(parts, came) for array in pair]
        step //= 2
    return parts


def first_hop(keep, send):
    return keep.astype(jnp.float32) + swap_with(send, 1).astype(jnp.float32)


def other_hops(totals):
    total = jnp.concatenate(totals, axis=1)
    count = total.shape[0]
    came = None
    while count > 1:
        count //= 2
        came = swap_with(total[count:].astype(jnp.bfloat16), 2 * count)
        total = total[:count] + came.astype(jnp.float32)
    return total[0], came


def scatter(part):
    return lax.psum_scatter(part, "dp", scatter_dimension=1, tiled=True)


def on_device(features, cotangent, factor_one, factor_two):
    owners = lax.axis_size("mp")
    shares = lax.axis_size("dp")
    held = factor_one.shape[0]
    half = held // 2
    unit = 8 if held % 16 == 0 else held
    units = held // unit

    position = jnp.full((1,), lax.axis_index("dp"), jnp.int32)
    parts = gathered_parts(factor_one[:unit])
    (head,) = first_head(position, features, parts, [(0, held)], owners, held)
    w_one = lax.all_gather(after(factor_one, head), "dp", axis=1, tiled=True)
    w_two = lax.all_gather(after(factor_two, w_one), "dp", axis=1, tiled=True)
    latest = arrived = exchange(head)
    received = [[(arrived, 0)], [(arrived, 0)]]
    if units > 1:
        cuts = [(0, half), (half, held)]
        rest = first_parts(
            after(features, head), w_one, unit, cuts, owners, held, 1, units - 1
        )
        for index, array in enumerate(rest):
            latest = exchange(array, latest)
            received[index].append((latest, index * half))

    backs = [units - 1, 1] if units > 1 else [1]
    layer, part_low, back_low = middle_part(
        received[0], w_two, features, cotangent, None, 0, half, [units]
    )
    latest = back_low = exchange(back_low, latest)
    layer, part_high, *back_high = middle_part(
        received[1], w_two, features, cotangent, layer, half, held, backs
    )
    grad_two = jnp.concatenate([scatter(part_low), scatter(part_high)], axis=0).astype(
        jnp.float32
    )
    for index, array in enumerate(back_high):
        before = (latest, grad_two) if index else latest
        latest = back_high[index] = exchange(array, before)

    grad, hops, parts_one, came = None, [], [], None
    for index in range(units):
        final = units > 1 and index == units - 1
        back, at = (back_high[1], 0) if final else (back_high[0], index)
        if final:
            back = after(back, parts_one[0])
        returned = [(back_low, index), (back, at)]
        grad_of = (w_one, cotangent)
        if final:
            keep, send = last_part(position, returned, index, features, None, None, shares)
            (grad,) = last_part(position, returned, index, None, grad_of, grad, shares)
        else:
            keep, send, grad = last_part(
                position, returned, index, features, grad_of, grad, shares
            )
        if came is not None:
            send = after(send, came)
        hops.append(first_hop(keep, send))
        if index >= units - 3 and index > 0 or units == 1:
            part, came = other_hops(hops)
            parts_one.append(part)
            hops = []
    return (
        layer,
        grad,
        jnp.concatenate(parts_one, axis=0),
        grad_two,
    )


def solution(mesh):
    in_specs = (P("dp", "mp"), P("dp", "mp"), P("mp", "dp", None), P("mp", "dp", None))
    out_specs = (P("dp", "mp"), P("dp", "mp"), P("mp", "dp", None), P("mp", "dp", None))
    return jax.shard_map(
        on_device, mesh=mesh, in_specs=in_specs, out_specs=out_specs, check_vma=False
    )
```

```python
import functools
import math

import jax
import jax.numpy as jnp
from jax import lax
from jax.experimental import pallas as pl
from jax.experimental.pallas import tpu as pltpu
from jax.sharding import PartitionSpec as P

LANES = 128
VMEM_LIMIT = 125 * 512 * 1024
GELU_SCALE = math.sqrt(2.0 / math.pi)


def contract(left, right, left_axis, right_axis):
    return lax.dot_general(
        left, right, (((left_axis,), (right_axis,)), ((), ())), preferred_element_type=jnp.float32
    )


def first_rows(feat_ref, weight, out_refs, unit, cuts, owners, held, swap):
    tokens = feat_ref.shape[0]
    group, width, _ = weight.shape
    for b in range(group):
        rows = contract(weight[b], feat_ref[:, b * width : (b + 1) * width], 1, 1)
        for lane in range(tokens // LANES):
            swap[lane, pl.ds(b, width, stride=group), :] = rows[
                :, lane * LANES : (lane + 1) * LANES
            ]
    for out_ref, (low, high) in zip(out_refs, cuts):
        for owner in range(owners):
            start = (owner * held + low) * group
            for lane in range(tokens // LANES):
                block = swap[lane, pl.ds(start, (high - low) * group), :]
                out_ref[owner, unit, :, :, lane * LANES : (lane + 1) * LANES] = block.reshape(
                    high - low, group, LANES
                ).astype(jnp.bfloat16)


def first_kernel(cuts, owners, held, units, *refs):
    feat_refs, w_refs, out_refs = refs[:units], refs[units : 2 * units], refs[2 * units : -2]
    weight, swap = refs[-2:]

    @pl.when(pl.program_id(0) == 0)
    def _():
        for unit, w_ref in enumerate(w_refs):
            for b in range(w_ref.shape[0]):
                weight[unit, b] = w_ref[b].T

    for unit in range(units):
        first_rows(feat_refs[unit], weight.at[unit], out_refs, unit, cuts, owners, held, swap)


def head_kernel(cuts, owners, held, shares, position_ref, feat_ref, *refs):
    part_refs, gathered, weight, swap = refs[:shares], *refs[-3:]
    rows = weight.shape[1] // shares

    @pl.when(pl.program_id(0) == 0)
    def _():
        for step, part_ref in enumerate(part_refs):
            start = pl.multiple_of((position_ref[0] ^ step) * rows, rows)
            gathered[:, pl.ds(start, rows), :] = part_ref[...]
        for b in range(weight.shape[0]):
            weight[b] = gathered[b].T

    first_rows(feat_ref, weight, refs[shares:-3], 0, cuts, owners, held, swap)


def first_call(features, group, width, cuts, owners, begin, units):
    tokens = features.shape[0]
    tile = min(256, tokens)
    outs = [
        jax.ShapeDtypeStruct((owners, units, high - low, group, tokens), jnp.bfloat16)
        for low, high in cuts
    ]
    moved = 2 * units * (tokens * group * width + group * width * width)
    moved += sum(2 * math.prod(out.shape) for out in outs)
    feat_specs = [
        pl.BlockSpec((tile, group * width), functools.partial(lambda u, t, *_: (t, u), begin + u))
        for u in range(units)
    ]
    out_specs = [
        pl.BlockSpec((owners, units, high - low, group, tile), lambda t, *_: (0, 0, 0, 0, t))
        for low, high in cuts
    ]
    swap = pltpu.VMEM((tile // LANES, width * group, LANES), jnp.float32)
    params = dict(
        out_shape=outs,
        compiler_params=pltpu.CompilerParams(vmem_limit_bytes=VMEM_LIMIT),
        cost_estimate=pl.CostEstimate(
            flops=2 * units * tokens * group * width * width,
            bytes_accessed=moved,
            transcendentals=0,
        ),
        name="first",
    )
    return (tokens // tile,), feat_specs, out_specs, swap, params


def first_parts(features, w_one, group, cuts, owners, held, begin, units):
    width = w_one.shape[1]
    grid, feat_specs, out_specs, swap, params = first_call(
        features, group, width, cuts, owners, begin, units
    )
    w_specs = [
        pl.BlockSpec((group, width, width), functools.partial(lambda u, t: (u, 0, 0), begin + u))
        for u in range(units)
    ]
    return pl.pallas_call(
        functools.partial(first_kernel, cuts, owners, held, units),
        grid=grid,
        in_specs=feat_specs + w_specs,
        out_specs=out_specs,
        scratch_shapes=[pltpu.VMEM((units, group, width, width), jnp.bfloat16), swap],
        **params,
    )(*[features] * units, *[w_one] * units)


def first_head(position, features, parts, cuts, owners, held):
    group, rows, width = parts[0].shape
    shares = len(parts)
    grid, feat_specs, out_specs, swap, params = first_call(
        features, group, width, cuts, owners, 0, 1
    )
    return pl.pallas_call(
        functools.partial(head_kernel, cuts, owners, held, shares),
        grid_spec=pltpu.PrefetchScalarGridSpec(
            num_scalar_prefetch=1,
            grid=grid,
            in_specs=feat_specs
            + [pl.BlockSpec((group, rows, width), lambda t, _: (0, 0, 0))] * shares,
            out_specs=out_specs,
            scratch_shapes=[pltpu.VMEM((group, width, width), jnp.bfloat16)] * 2 + [swap],
        ),
        **params,
    )(position, features, *parts)


def middle_kernel(owners, group, sources, backs, tile, chained, *refs):
    r_refs = refs[: len(sources)]
    w_ref, feat_ref, cot_ref = refs[len(sources) : len(sources) + 3]
    outs = refs[len(sources) + 3 + chained :]
    layer_ref, part_ref, back_refs = outs[0], outs[1], outs[2:]
    weight = w_ref[0]
    tokens = feat_ref.shape[0]
    depth = weight.shape[0]
    part = None
    for begin in range(0, tokens, tile):
        span = slice(begin, begin + tile)
        first = jnp.concatenate(
            [
                ref[:, unit, 0, :, span].astype(jnp.float32)
                for ref, units in zip(r_refs, sources)
                for unit in range(units)
            ],
            axis=1,
        )
        first = first.reshape(depth, tile).astype(jnp.bfloat16)
        value = contract(first, weight, 0, 0)
        square = value * value
        tangent = jnp.tanh(GELU_SCALE * (value + 0.044715 * square * value))
        half = 0.5 * (1.0 + tangent)
        layer_ref[span, :] = (feat_ref[span, :].astype(jnp.float32) + value * half).astype(
            jnp.bfloat16
        )
        rate = half + 0.5 * value * (1.0 - tangent * tangent) * GELU_SCALE * (
            1.0 + 3.0 * 0.044715 * square
        )
        slope = (cot_ref[span, :].astype(jnp.float32) * rate).astype(jnp.bfloat16)
        back = contract(weight, slope, 1, 1).reshape(owners, depth // owners, tile)
        start = 0
        for units, back_ref in zip(backs, back_refs):
            for unit in range(units):
                back_ref[:, unit, 0, :, span] = back[:, start : start + group].astype(jnp.bfloat16)
                start += group
        term = contract(first, slope, 1, 0)
        part = term if part is None else part + term
    part_ref[0] = part.astype(jnp.bfloat16)


def middle_part(received, w_two, features, cotangent, layer, low, high, backs):
    tokens, columns = features.shape
    owners, _, _, group, _ = received[0][0].shape
    count = high - low
    depth, width = w_two.shape[1:]
    tile = min(256, tokens)
    chained = 0 if layer is None else 1
    column = pl.BlockSpec((tokens, width), lambda j: (0, low + j))
    sources = [array.shape[1] for array, _ in received]
    operands = [array for array, _ in received] + [w_two, features, cotangent]
    operands += [layer] if chained else []

    def spec(units, skipped):
        return pl.BlockSpec(
            (owners, units, 1, group, tokens), lambda j: (0, 0, low - skipped + j, 0, 0)
        )

    return pl.pallas_call(
        functools.partial(middle_kernel, owners, group, sources, backs, tile, chained),
        grid=(count,),
        in_specs=[spec(array.shape[1], skipped) for array, skipped in received]
        + [pl.BlockSpec((1, depth, width), lambda j: (low + j, 0, 0)), column, column]
        + [pl.BlockSpec(memory_space=pl.ANY)] * chained,
        out_specs=[column, pl.BlockSpec((1, depth, width), lambda j: (j, 0, 0))]
        + [spec(units, low) for units in backs],
        out_shape=[
            jax.ShapeDtypeStruct((tokens, columns), jnp.bfloat16),
            jax.ShapeDtypeStruct((count, depth, width), jnp.bfloat16),
        ]
        + [
            jax.ShapeDtypeStruct((owners, units, count, group, tokens), jnp.bfloat16)
            for units in backs
        ],
        input_output_aliases={len(operands) - 1: 0} if chained else {},
        compiler_params=pltpu.CompilerParams(vmem_limit_bytes=VMEM_LIMIT),
        cost_estimate=pl.CostEstimate(
            flops=6 * count * tokens * depth * width,
            bytes_accessed=count * (10 * tokens * width + 4 * depth * width),
            transcendentals=count * tokens * width,
        ),
        name="middle",
    )(*operands)


def last_kernel(held, sources, shares, rows_out, grad_out, chained, position_ref, *refs):
    q_refs, refs = refs[: len(sources)], list(refs[len(sources) :])
    feat_ref = refs.pop(0) if rows_out else None
    w_ref, cot_ref = (refs.pop(0), refs.pop(0)) if grad_out else (None, None)
    refs = refs[chained:]
    keep_ref, send_ref = (refs.pop(0), refs.pop(0)) if rows_out else (None, None)
    grad_ref = refs.pop(0) if grad_out else None
    swap = refs.pop(0)
    total = refs.pop(0) if rows_out else None
    group, tokens = q_refs[0].shape[3:]
    width = swap.shape[1] // group
    lanes = tokens // LANES
    step = pl.program_id(0)

    if rows_out:

        @pl.when(step == 0)
        def _():
            total[...] = jnp.zeros_like(total)

    for q_ref, (low, high) in zip(q_refs, sources):
        for owner in range(q_ref.shape[0]):
            start = (owner * held + low) * group
            for lane in range(lanes):
                block = q_ref[owner, 0, :, :, lane * LANES : (lane + 1) * LANES]
                swap[lane, pl.ds(start, (high - low) * group), :] = block.astype(
                    jnp.float32
                ).reshape((high - low) * group, LANES)
    for b in range(group):
        back = jnp.concatenate(
            [swap[lane, pl.ds(b, width, stride=group), :] for lane in range(lanes)], axis=1
        ).astype(jnp.bfloat16)
        columns = slice(b * width, (b + 1) * width)
        if grad_out:
            through = contract(back, w_ref[b], 0, 1)
            grad_ref[:, columns] = (cot_ref[:, columns].astype(jnp.float32) + through).astype(
                jnp.bfloat16
            )
        if rows_out:
            total[b] += contract(back, feat_ref[:, columns], 1, 0)

    if rows_out:

        @pl.when(step == pl.num_programs(0) - 1)
        def _():
            rows = width // shares
            me = position_ref[0]
            for parity in range(2):

                @pl.when((me & 1) == parity)
                def _():
                    for b in range(group):
                        part = total[b].T.astype(jnp.bfloat16)
                        for share in range(shares):
                            ref = keep_ref if share & 1 == parity else send_ref
                            ref[(me >> 1) ^ (share >> 1), b] = part[
                                share * rows : (share + 1) * rows
                            ]


def last_part(position, returned, unit, rows_of, grad_of, grad, shares):
    tokens = returned[0][0].shape[-1]
    owners, _, _, group, _ = returned[0][0].shape
    held = sum(array.shape[2] for array, _ in returned)
    width = owners * held
    tile = min(256, tokens)
    strip = pl.BlockSpec((tile, group * width), lambda t, _: (t, unit))
    operands, specs, sources, low = [], [], [], 0
    for array, at in returned:
        count = array.shape[2]
        index_map = functools.partial(lambda at, t, _: (0, at, 0, 0, t), at)
        operands.append(array)
        specs.append(pl.BlockSpec((owners, 1, count, group, tile), index_map))
        sources.append((low, low + count))
        low += count
    outs, out_specs, aliases = [], [], {}
    scratch = [pltpu.VMEM((tile // LANES, width * group, LANES), jnp.float32)]
    chained = 1 if grad_of is not None and grad is not None else 0
    if rows_of is not None:
        operands.append(rows_of)
        specs.append(strip)
        block = (shares // 2, group, width // shares, width)
        outs += [jax.ShapeDtypeStruct(block, jnp.bfloat16)] * 2
        out_specs += [pl.BlockSpec(block, lambda t, _: (0, 0, 0, 0))] * 2
        scratch.append(pltpu.VMEM((group, width, width), jnp.float32))
    if grad_of is not None:
        w_one, cotangent = grad_of
        operands += [w_one, cotangent]
        specs += [pl.BlockSpec((group, width, width), lambda t, _: (unit, 0, 0)), strip]
        if chained:
            operands.append(grad)
            specs.append(pl.BlockSpec(memory_space=pl.ANY))
            aliases = {len(operands): len(outs)}
        outs.append(jax.ShapeDtypeStruct(cotangent.shape, jnp.bfloat16))
        out_specs.append(strip)
    jobs = (rows_of is not None) + (grad_of is not None)
    return pl.pallas_call(
        functools.partial(
            last_kernel, held, sources, shares, rows_of is not None, grad_of is not None, chained
        ),
        grid_spec=pltpu.PrefetchScalarGridSpec(
            num_scalar_prefetch=1,
            grid=(tokens // tile,),
            in_specs=specs,
            out_specs=out_specs,
            scratch_shapes=scratch,
        ),
        out_shape=outs,
        input_output_aliases=aliases,
        compiler_params=pltpu.CompilerParams(vmem_limit_bytes=VMEM_LIMIT),
        cost_estimate=pl.CostEstimate(
            flops=2 * jobs * group * tokens * width * width,
            bytes_accessed=group * (2 + 3 * jobs) * tokens * width,
            transcendentals=0,
        ),
        name="last",
    )(position, *operands)


def exchange(array, before=None):
    if before is not None:
        array = after(array, before)
    return lax.all_to_all(array, "mp", split_axis=0, concat_axis=0, tiled=True)


def after(array, before):
    return lax.optimization_barrier((array, before))[0]


def swap_with(array, step):
    size = lax.axis_size("dp")
    return lax.ppermute(array, "dp", [(d, d ^ step) for d in range(size)])


def gathered_parts(part):
    parts = [part]
    step = lax.axis_size("dp") // 2
    while step:
        came = [swap_with(array, step) for array in parts]
        parts = [array for pair in zip(parts, came) for array in pair]
        step //= 2
    return parts


def first_hop(keep, send):
    return [keep, swap_with(send, 1)]


def added(terms):
    return sum((term.astype(jnp.float32) for term in terms[1:]), terms[0].astype(jnp.float32))


def other_hops(sums):
    group = sums[0][0].shape[1]
    count = sums[0][0].shape[0]
    came = None
    while count > 1:
        count //= 2
        leaving = [added([term[count:] for term in terms]).astype(jnp.bfloat16) for terms in sums]
        came = swap_with(jnp.concatenate(leaving, axis=1), 2 * count)
        sums = [
            [term[:count] for term in terms] + [came[:, at * group : (at + 1) * group]]
            for at, terms in enumerate(sums)
        ]
    return [added([term[0] for term in terms]) for terms in sums], came


def scatter(part):
    return lax.psum_scatter(part, "dp", scatter_dimension=1, tiled=True)


def on_device(features, cotangent, factor_one, factor_two):
    owners = lax.axis_size("mp")
    shares = lax.axis_size("dp")
    held = factor_one.shape[0]
    half = held // 2
    unit = 8 if held % 16 == 0 else held
    units = held // unit

    position = jnp.full((1,), lax.axis_index("dp"), jnp.int32)
    parts = gathered_parts(factor_one[:unit])
    (head,) = first_head(position, features, parts, [(0, held)], owners, held)
    w_one = lax.all_gather(after(factor_one, head), "dp", axis=1, tiled=True)
    w_two = lax.all_gather(after(factor_two, w_one), "dp", axis=1, tiled=True)
    latest = arrived = exchange(head)
    received = [[(arrived, 0)], [(arrived, 0)]]
    if units > 1:
        cuts = [(0, half), (half, held)]
        rest = first_parts(
            after(features, head), w_one, unit, cuts, owners, held, 1, units - 1
        )
        for index, array in enumerate(rest):
            latest = exchange(array, latest)
            received[index].append((latest, index * half))

    backs = [units - 1, 1] if units > 1 else [1]
    layer, part_low, back_low = middle_part(
        received[0], w_two, features, cotangent, None, 0, half, [units]
    )
    latest = back_low = exchange(back_low, latest)
    layer, part_high, *back_high = middle_part(
        received[1], w_two, features, cotangent, layer, half, held, backs
    )
    grad_two = jnp.concatenate([scatter(part_low), scatter(part_high)], axis=0).astype(
        jnp.float32
    )
    for index, array in enumerate(back_high):
        before = (latest, grad_two) if index else latest
        latest = back_high[index] = exchange(array, before)

    grad, hops, parts_one, came = None, [], [], None
    for index in range(units):
        final = units > 1 and index == units - 1
        back, at = (back_high[1], 0) if final else (back_high[0], index)
        returned = [(back_low, index), (back, at)]
        grad_of = (w_one, cotangent)
        if final:
            keep, send = last_part(position, returned, index, features, None, None, shares)
            (grad,) = last_part(position, returned, index, None, grad_of, grad, shares)
        else:
            keep, send, grad = last_part(
                position, returned, index, features, grad_of, grad, shares
            )
        if came is not None:
            send = after(send, came)
        hops.append(first_hop(keep, send))
        if index >= units - 3 and index > 0 or units == 1:
            parts, came = other_hops(hops)
            parts_one += parts
            hops = []
    empty = jnp.zeros((held,) + parts_one[0].shape[1:], jnp.float32)
    grad_one = after(empty, back_low)
    for index, part in enumerate(parts_one):
        grad_one = lax.dynamic_update_slice(grad_one, part, (index * unit, 0, 0))
    return (
        layer,
        grad,
        grad_one,
        grad_two,
    )


def solution(mesh):
    in_specs = (P("dp", "mp"), P("dp", "mp"), P("mp", "dp", None), P("mp", "dp", None))
    out_specs = (P("dp", "mp"), P("dp", "mp"), P("mp", "dp", None), P("mp", "dp", None))
    return jax.shard_map(
        on_device, mesh=mesh, in_specs=in_specs, out_specs=out_specs, check_vma=False
    )
```

```python
import functools
import math

import jax
import jax.numpy as jnp
from jax import lax
from jax.experimental import pallas as pl
from jax.experimental.pallas import tpu as pltpu
from jax.sharding import PartitionSpec as P

LANES = 128
VMEM_LIMIT = 125 * 512 * 1024
GELU_SCALE = math.sqrt(2.0 / math.pi)


def contract(left, right, left_axis, right_axis):
    return lax.dot_general(
        left, right, (((left_axis,), (right_axis,)), ((), ())), preferred_element_type=jnp.float32
    )


def first_rows(feat_ref, weight, out_refs, unit, cuts, owners, held, swap):
    tokens = feat_ref.shape[0]
    group, width, _ = weight.shape
    for b in range(group):
        rows = contract(weight[b], feat_ref[:, b * width : (b + 1) * width], 1, 1)
        for lane in range(tokens // LANES):
            swap[lane, pl.ds(b, width, stride=group), :] = rows[
                :, lane * LANES : (lane + 1) * LANES
            ]
    for out_ref, (low, high) in zip(out_refs, cuts):
        for owner in range(owners):
            start = (owner * held + low) * group
            for lane in range(tokens // LANES):
                block = swap[lane, pl.ds(start, (high - low) * group), :]
                out_ref[owner, unit, :, :, lane * LANES : (lane + 1) * LANES] = block.reshape(
                    high - low, group, LANES
                ).astype(jnp.bfloat16)


def first_kernel(cuts, owners, held, units, *refs):
    feat_refs, w_refs, out_refs = refs[:units], refs[units : 2 * units], refs[2 * units : -2]
    weight, swap = refs[-2:]

    @pl.when(pl.program_id(0) == 0)
    def _():
        for unit, w_ref in enumerate(w_refs):
            for b in range(w_ref.shape[0]):
                weight[unit, b] = w_ref[b].T

    for unit in range(units):
        first_rows(feat_refs[unit], weight.at[unit], out_refs, unit, cuts, owners, held, swap)


def head_kernel(cuts, owners, held, shares, position_ref, feat_ref, *refs):
    part_refs, gathered, weight, swap = refs[:shares], *refs[-3:]
    rows = weight.shape[1] // shares

    @pl.when(pl.program_id(0) == 0)
    def _():
        for step, part_ref in enumerate(part_refs):
            start = pl.multiple_of((position_ref[0] ^ step) * rows, rows)
            gathered[:, pl.ds(start, rows), :] = part_ref[...]
        for b in range(weight.shape[0]):
            weight[b] = gathered[b].T

    first_rows(feat_ref, weight, refs[shares:-3], 0, cuts, owners, held, swap)


def first_call(features, group, width, cuts, owners, begin, units):
    tokens = features.shape[0]
    tile = min(256, tokens)
    outs = [
        jax.ShapeDtypeStruct((owners, units, high - low, group, tokens), jnp.bfloat16)
        for low, high in cuts
    ]
    moved = 2 * units * (tokens * group * width + group * width * width)
    moved += sum(2 * math.prod(out.shape) for out in outs)
    feat_specs = [
        pl.BlockSpec((tile, group * width), functools.partial(lambda u, t, *_: (t, u), begin + u))
        for u in range(units)
    ]
    out_specs = [
        pl.BlockSpec((owners, units, high - low, group, tile), lambda t, *_: (0, 0, 0, 0, t))
        for low, high in cuts
    ]
    swap = pltpu.VMEM((tile // LANES, width * group, LANES), jnp.float32)
    params = dict(
        out_shape=outs,
        compiler_params=pltpu.CompilerParams(vmem_limit_bytes=VMEM_LIMIT),
        cost_estimate=pl.CostEstimate(
            flops=2 * units * tokens * group * width * width,
            bytes_accessed=moved,
            transcendentals=0,
        ),
        name="first",
    )
    return (tokens // tile,), feat_specs, out_specs, swap, params


def first_parts(features, w_one, group, cuts, owners, held, begin, units):
    width = w_one.shape[1]
    grid, feat_specs, out_specs, swap, params = first_call(
        features, group, width, cuts, owners, begin, units
    )
    w_specs = [
        pl.BlockSpec((group, width, width), functools.partial(lambda u, t: (u, 0, 0), begin + u))
        for u in range(units)
    ]
    return pl.pallas_call(
        functools.partial(first_kernel, cuts, owners, held, units),
        grid=grid,
        in_specs=feat_specs + w_specs,
        out_specs=out_specs,
        scratch_shapes=[pltpu.VMEM((units, group, width, width), jnp.bfloat16), swap],
        **params,
    )(*[features] * units, *[w_one] * units)


def first_head(position, features, parts, cuts, owners, held):
    group, rows, width = parts[0].shape
    shares = len(parts)
    grid, feat_specs, out_specs, swap, params = first_call(
        features, group, width, cuts, owners, 0, 1
    )
    return pl.pallas_call(
        functools.partial(head_kernel, cuts, owners, held, shares),
        grid_spec=pltpu.PrefetchScalarGridSpec(
            num_scalar_prefetch=1,
            grid=grid,
            in_specs=feat_specs
            + [pl.BlockSpec((group, rows, width), lambda t, _: (0, 0, 0))] * shares,
            out_specs=out_specs,
            scratch_shapes=[pltpu.VMEM((group, width, width), jnp.bfloat16)] * 2 + [swap],
        ),
        **params,
    )(position, features, *parts)


def middle_kernel(owners, group, sources, backs, tile, chained, *refs):
    r_refs = refs[: len(sources)]
    w_ref, feat_ref, cot_ref = refs[len(sources) : len(sources) + 3]
    outs = refs[len(sources) + 3 + chained :]
    layer_ref, part_ref, back_refs = outs[0], outs[1], outs[2:]
    weight = w_ref[0]
    tokens = feat_ref.shape[0]
    depth = weight.shape[0]
    part = None
    for begin in range(0, tokens, tile):
        span = slice(begin, begin + tile)
        first = jnp.concatenate(
            [
                ref[:, unit, 0, :, span].astype(jnp.float32)
                for ref, units in zip(r_refs, sources)
                for unit in range(units)
            ],
            axis=1,
        )
        first = first.reshape(depth, tile).astype(jnp.bfloat16)
        value = contract(first, weight, 0, 0)
        square = value * value
        tangent = jnp.tanh(GELU_SCALE * (value + 0.044715 * square * value))
        half = 0.5 * (1.0 + tangent)
        layer_ref[span, :] = (feat_ref[span, :].astype(jnp.float32) + value * half).astype(
            jnp.bfloat16
        )
        rate = half + 0.5 * value * (1.0 - tangent * tangent) * GELU_SCALE * (
            1.0 + 3.0 * 0.044715 * square
        )
        slope = (cot_ref[span, :].astype(jnp.float32) * rate).astype(jnp.bfloat16)
        back = contract(weight, slope, 1, 1).reshape(owners, depth // owners, tile)
        start = 0
        for units, back_ref in zip(backs, back_refs):
            for unit in range(units):
                back_ref[:, unit, 0, :, span] = back[:, start : start + group].astype(jnp.bfloat16)
                start += group
        term = contract(first, slope, 1, 0)
        part = term if part is None else part + term
    part_ref[0] = part.astype(jnp.bfloat16)


def middle_part(received, w_two, features, cotangent, layer, low, high, backs):
    tokens, columns = features.shape
    owners, _, _, group, _ = received[0][0].shape
    count = high - low
    depth, width = w_two.shape[1:]
    tile = min(256, tokens)
    chained = 0 if layer is None else 1
    column = pl.BlockSpec((tokens, width), lambda j: (0, low + j))
    sources = [array.shape[1] for array, _ in received]
    operands = [array for array, _ in received] + [w_two, features, cotangent]
    operands += [layer] if chained else []

    def spec(units, skipped):
        return pl.BlockSpec(
            (owners, units, 1, group, tokens), lambda j: (0, 0, low - skipped + j, 0, 0)
        )

    return pl.pallas_call(
        functools.partial(middle_kernel, owners, group, sources, backs, tile, chained),
        grid=(count,),
        in_specs=[spec(array.shape[1], skipped) for array, skipped in received]
        + [pl.BlockSpec((1, depth, width), lambda j: (low + j, 0, 0)), column, column]
        + [pl.BlockSpec(memory_space=pl.ANY)] * chained,
        out_specs=[column, pl.BlockSpec((1, depth, width), lambda j: (j, 0, 0))]
        + [spec(units, low) for units in backs],
        out_shape=[
            jax.ShapeDtypeStruct((tokens, columns), jnp.bfloat16),
            jax.ShapeDtypeStruct((count, depth, width), jnp.bfloat16),
        ]
        + [
            jax.ShapeDtypeStruct((owners, units, count, group, tokens), jnp.bfloat16)
            for units in backs
        ],
        input_output_aliases={len(operands) - 1: 0} if chained else {},
        compiler_params=pltpu.CompilerParams(vmem_limit_bytes=VMEM_LIMIT),
        cost_estimate=pl.CostEstimate(
            flops=6 * count * tokens * depth * width,
            bytes_accessed=count * (10 * tokens * width + 4 * depth * width),
            transcendentals=count * tokens * width,
        ),
        name="middle",
    )(*operands)


def last_kernel(held, sources, shares, rows_out, grad_out, chained, position_ref, *refs):
    q_refs, refs = refs[: len(sources)], list(refs[len(sources) :])
    feat_ref = refs.pop(0) if rows_out else None
    w_ref, cot_ref = (refs.pop(0), refs.pop(0)) if grad_out else (None, None)
    refs = refs[chained:]
    keep_ref, send_ref = (refs.pop(0), refs.pop(0)) if rows_out else (None, None)
    grad_ref = refs.pop(0) if grad_out else None
    swap = refs.pop(0)
    total = refs.pop(0) if rows_out else None
    group, tokens = q_refs[0].shape[3:]
    width = swap.shape[1] // group
    lanes = tokens // LANES
    step = pl.program_id(0)

    if rows_out:

        @pl.when(step == 0)
        def _():
            total[...] = jnp.zeros_like(total)

    for q_ref, (low, high) in zip(q_refs, sources):
        for owner in range(q_ref.shape[0]):
            start = (owner * held + low) * group
            for lane in range(lanes):
                block = q_ref[owner, 0, :, :, lane * LANES : (lane + 1) * LANES]
                swap[lane, pl.ds(start, (high - low) * group), :] = block.astype(
                    jnp.float32
                ).reshape((high - low) * group, LANES)
    for b in range(group):
        back = jnp.concatenate(
            [swap[lane, pl.ds(b, width, stride=group), :] for lane in range(lanes)], axis=1
        ).astype(jnp.bfloat16)
        columns = slice(b * width, (b + 1) * width)
        if grad_out:
            through = contract(back, w_ref[b], 0, 1)
            grad_ref[:, columns] = (cot_ref[:, columns].astype(jnp.float32) + through).astype(
                jnp.bfloat16
            )
        if rows_out:
            total[b] += contract(back, feat_ref[:, columns], 1, 0)

    if rows_out:

        @pl.when(step == pl.num_programs(0) - 1)
        def _():
            rows = width // shares
            me = position_ref[0]
            for parity in range(2):

                @pl.when((me & 1) == parity)
                def _():
                    for b in range(group):
                        part = total[b].T.astype(jnp.bfloat16)
                        for share in range(shares):
                            ref = keep_ref if share & 1 == parity else send_ref
                            ref[(me >> 1) ^ (share >> 1), b] = part[
                                share * rows : (share + 1) * rows
                            ]


def last_part(position, returned, unit, rows_of, grad_of, grad, shares):
    tokens = returned[0][0].shape[-1]
    owners, _, _, group, _ = returned[0][0].shape
    held = sum(array.shape[2] for array, _ in returned)
    width = owners * held
    tile = min(256, tokens)
    strip = pl.BlockSpec((tile, group * width), lambda t, _: (t, unit))
    operands, specs, sources, low = [], [], [], 0
    for array, at in returned:
        count = array.shape[2]
        index_map = functools.partial(lambda at, t, _: (0, at, 0, 0, t), at)
        operands.append(array)
        specs.append(pl.BlockSpec((owners, 1, count, group, tile), index_map))
        sources.append((low, low + count))
        low += count
    outs, out_specs, aliases = [], [], {}
    scratch = [pltpu.VMEM((tile // LANES, width * group, LANES), jnp.float32)]
    chained = 1 if grad_of is not None and grad is not None else 0
    if rows_of is not None:
        operands.append(rows_of)
        specs.append(strip)
        block = (shares // 2, group, width // shares, width)
        outs += [jax.ShapeDtypeStruct(block, jnp.bfloat16)] * 2
        out_specs += [pl.BlockSpec(block, lambda t, _: (0, 0, 0, 0))] * 2
        scratch.append(pltpu.VMEM((group, width, width), jnp.float32))
    if grad_of is not None:
        w_one, cotangent = grad_of
        operands += [w_one, cotangent]
        specs += [pl.BlockSpec((group, width, width), lambda t, _: (unit, 0, 0)), strip]
        if chained:
            operands.append(grad)
            specs.append(pl.BlockSpec(memory_space=pl.ANY))
            aliases = {len(operands): len(outs)}
        outs.append(jax.ShapeDtypeStruct(cotangent.shape, jnp.bfloat16))
        out_specs.append(strip)
    jobs = (rows_of is not None) + (grad_of is not None)
    return pl.pallas_call(
        functools.partial(
            last_kernel, held, sources, shares, rows_of is not None, grad_of is not None, chained
        ),
        grid_spec=pltpu.PrefetchScalarGridSpec(
            num_scalar_prefetch=1,
            grid=(tokens // tile,),
            in_specs=specs,
            out_specs=out_specs,
            scratch_shapes=scratch,
        ),
        out_shape=outs,
        input_output_aliases=aliases,
        compiler_params=pltpu.CompilerParams(vmem_limit_bytes=VMEM_LIMIT),
        cost_estimate=pl.CostEstimate(
            flops=2 * jobs * group * tokens * width * width,
            bytes_accessed=group * (2 + 3 * jobs) * tokens * width,
            transcendentals=0,
        ),
        name="last",
    )(position, *operands)


def exchange(array, before=None):
    if before is not None:
        array = after(array, before)
    return lax.all_to_all(array, "mp", split_axis=0, concat_axis=0, tiled=True)


def after(array, before):
    return lax.optimization_barrier((array, before))[0]


def swap_with(array, step):
    size = lax.axis_size("dp")
    return lax.ppermute(array, "dp", [(d, d ^ step) for d in range(size)])


def gathered_parts(part):
    parts = [part]
    step = lax.axis_size("dp") // 2
    while step:
        came = [swap_with(array, step) for array in parts]
        parts = [array for pair in zip(parts, came) for array in pair]
        step //= 2
    return parts


def first_hop(keep, send):
    return [keep, swap_with(send, 1)]


def added(terms):
    return sum((term.astype(jnp.float32) for term in terms[1:]), terms[0].astype(jnp.float32))


def other_hops(sums):
    group = sums[0][0].shape[1]
    count = sums[0][0].shape[0]
    came = None
    while count > 1:
        count //= 2
        leaving = [added([term[count:] for term in terms]).astype(jnp.bfloat16) for terms in sums]
        came = swap_with(jnp.concatenate(leaving, axis=1), 2 * count)
        sums = [
            [term[:count] for term in terms] + [came[:, at * group : (at + 1) * group]]
            for at, terms in enumerate(sums)
        ]
    return [added([term[0] for term in terms]) for terms in sums], came


def scatter(part):
    return lax.psum_scatter(part, "dp", scatter_dimension=1, tiled=True)


def on_device(features, cotangent, factor_one, factor_two):
    owners = lax.axis_size("mp")
    shares = lax.axis_size("dp")
    held = factor_one.shape[0]
    half = held // 2
    unit = 8 if held % 16 == 0 else held
    units = held // unit

    position = jnp.full((1,), lax.axis_index("dp"), jnp.int32)
    parts = gathered_parts(factor_one[:unit])
    (head,) = first_head(position, features, parts, [(0, held)], owners, held)
    w_one = lax.all_gather(after(factor_one, head), "dp", axis=1, tiled=True)
    w_two = lax.all_gather(after(factor_two, w_one), "dp", axis=1, tiled=True)
    latest = arrived = exchange(head)
    received = [[(arrived, 0)], [(arrived, 0)]]
    if units > 1:
        cuts = [(0, half), (half, held)]
        rest = first_parts(
            after(features, head), w_one, unit, cuts, owners, held, 1, units - 1
        )
        for index, array in enumerate(rest):
            latest = exchange(array, latest)
            received[index].append((latest, index * half))

    backs = [units - 1, 1] if units > 1 else [1]
    layer, part_low, back_low = middle_part(
        received[0], w_two, features, cotangent, None, 0, half, [units]
    )
    latest = back_low = exchange(back_low, latest)
    layer, part_high, *back_high = middle_part(
        received[1], w_two, features, cotangent, layer, half, held, backs
    )
    grad_two = jnp.concatenate([scatter(part_low), scatter(part_high)], axis=0).astype(
        jnp.float32
    )
    grad_one = factor_one.astype(jnp.float32)
    for index, array in enumerate(back_high):
        if index:
            array, grad_one, grad_two = lax.optimization_barrier((array, grad_one, grad_two))
        latest = back_high[index] = exchange(array, latest)

    grad, hops, parts_one, came = None, [], [], None
    for index in range(units):
        final = units > 1 and index == units - 1
        back, at = (back_high[1], 0) if final else (back_high[0], index)
        returned = [(back_low, index), (back, at)]
        grad_of = (w_one, cotangent)
        if final:
            grad_one = lax.dynamic_update_slice(grad_one, parts_one[0], (0, 0, 0))
            back = after(back, grad_one)
            returned = [(back_low, index), (back, at)]
            keep, send = last_part(position, returned, index, features, None, None, shares)
            (grad,) = last_part(position, returned, index, None, grad_of, grad, shares)
        else:
            keep, send, grad = last_part(
                position, returned, index, features, grad_of, grad, shares
            )
        if came is not None:
            send = after(send, came)
        hops.append(first_hop(keep, send))
        if index >= units - 3 and index > 0 or units == 1:
            parts, came = other_hops(hops)
            parts_one += parts
            hops = []
    for index, part in enumerate(parts_one):
        if index or units == 1:
            grad_one = lax.dynamic_update_slice(grad_one, part, (index * unit, 0, 0))
    return (
        layer,
        grad,
        grad_one,
        grad_two,
    )


def solution(mesh):
    in_specs = (P("dp", "mp"), P("dp", "mp"), P("mp", "dp", None), P("mp", "dp", None))
    out_specs = (P("dp", "mp"), P("dp", "mp"), P("mp", "dp", None), P("mp", "dp", None))
    return jax.shard_map(
        on_device, mesh=mesh, in_specs=in_specs, out_specs=out_specs, check_vma=False
    )
```
